128 devices in a mesh: tower: 4 (over x), dp: 8 (over y_lo, z), mp: 4 (over y_hi, core).
Axes of the slice: x: 4, y: 4 (y_hi: 2, y_lo: 2; y = y_hi * 2 + y_lo), z: 4, core: 2. Of those that a mesh axis runs over, the one named last changes fastest.
Arguments:
- image_in: bfloat16 [4, 1024, 1792], P('tower', 'dp', 'mp'), may hold values from -6 to 6
- text_in: bfloat16 [4, 3072, 1152], P('tower', 'dp', 'mp'), may hold values from -6 to 6
- img_w1: bfloat16 [1792, 7680], P(None, 'mp'), may hold values from -0.125 to 0.125
- img_w2: bfloat16 [7680, 1792], P('mp'), may hold values from -0.0625 to 0.0625
- img_proj: bfloat16 [1792, 1152], P(None, 'mp'), may hold values from -0.125 to 0.125
- txt_w1: bfloat16 [1152, 2560], P(None, 'mp'), may hold values from -0.1875 to 0.1875
- txt_w2: bfloat16 [2560, 1152], P('mp'), may hold values from -0.125 to 0.125
- label_offset: int32 [4, 8], P('tower', 'dp'), may hold values from 0 to 3071
- logit_scale: float32 [], replicated, may hold values from 64 to 72
- logit_bias: float32 [], replicated, may hold values from -10 to -8
- loss_scale: float32 [], replicated, may hold values from 2 to 8
Outputs:
- image_grad: float32 [4, 1024, 1792], P('tower', 'dp', 'mp')
- text_grad: float32 [4, 3072, 1152], P('tower', 'dp', 'mp')
- grad_img_w1: float32 [1792, 7680], P(('tower', 'dp'), 'mp')
- grad_img_w2: float32 [7680, 1792], P('mp', ('tower', 'dp'))
- grad_img_proj: float32 [1792, 1152], P(('tower', 'dp'), 'mp')
- grad_txt_w1: float32 [1152, 2560], P(('tower', 'dp'), 'mp')
- grad_txt_w2: float32 [2560, 1152], P('mp', ('tower', 'dp'))
The draws below stay inside these ranges and needn't reach their ends.
All inputs are finite; a program needn't handle non-finite values.
Results may differ from the reference program's by a relative error of at most 0.02.
Values may be sent and summed in bfloat16 or wider, within the bound.
A program may use at most 192 MiB of HBM per device.

```python
import math
import jax
import jax.numpy as jnp
from jax import lax

WI = 1792
FI = 7680
WT = 1152
FT = 2560
ROW_DEV = 128
ROWS_SEC = 1024
BATCH = 3072
N_TOWER = 4
N_DP = 8


def plant(values, rng, least, largest):
    longest = values.shape.index(max(values.shape))
    spots = []
    for shift in (0, 1):
        where = [jax.random.randint(jax.random.fold_in(rng, axis), (), 0, length) for axis, length in enumerate(values.shape)]
        where[longest] = (where[longest] + shift) % values.shape[longest]
        spots.append(tuple(where))
    return values.at[spots[0]].set(least).at[spots[1]].set(largest)


def shard_levels(rng, dims, cuts, smallest, high):
    gain, own = 1.0, jax.random.fold_in(rng, 6)
    for dim, blocks in cuts:
        draws = jnp.exp(jax.random.uniform(jax.random.fold_in(own, dim), (blocks,), jnp.float32, smallest / len(cuts), high / len(cuts)))
        gain = gain * jnp.repeat(draws, dims[dim] // blocks).reshape([-1 if axis == dim else 1 for axis in range(len(dims))])
    return gain


def bell_draw(own_key, extent, deviation, reach, cuts=(), held_as=jnp.bfloat16):
    level = shard_levels(own_key, extent, cuts, -0.22, 0.18) if cuts else 1.0
    result = jax.random.normal(own_key, extent, jnp.float32) * deviation * level
    return jnp.minimum(jnp.maximum(result, -reach), reach).astype(held_as)


def setup_inputs(seed: int = 0) -> dict:
    key_list = jax.random.split(jax.random.key(seed), 12)
    return {
        "image_in": bell_draw(key_list[0], (N_TOWER, ROWS_SEC, WI), 1.0, 6.0, ((0, 4), (1, 8), (2, 4))),
        "text_in": bell_draw(key_list[1], (N_TOWER, BATCH, WT), 1.0, 6.0, ((0, 4), (1, 8), (2, 4))),
        "img_w1": bell_draw(key_list[2], (WI, FI), WI ** -0.5, 0.125, ((1, 4),)),
        "img_w2": bell_draw(key_list[3], (FI, WI), FI ** -0.5, 0.0625, ((0, 4),)),
        "img_proj": bell_draw(key_list[4], (WI, WT), WI ** -0.5, 0.125, ((1, 4),)),
        "txt_w1": bell_draw(key_list[5], (WT, FT), WT ** -0.5, 0.1875, ((1, 4),)),
        "txt_w2": bell_draw(key_list[6], (FT, WT), FT ** -0.5, 0.125, ((0, 4),)),
        "label_offset": plant(jax.random.randint(key_list[7], (N_TOWER, N_DP), 0, BATCH), jax.random.fold_in(key_list[7], 1), 0, BATCH - 1).astype(jnp.int32),
        "logit_scale": jnp.clip(jax.random.uniform(key_list[8], (), jnp.float32, 64.0, 72.0), 64.0, 72.0),
        "logit_bias": jnp.clip(jax.random.uniform(key_list[9], (), jnp.float32, -10.0, -8.0), -10.0, -8.0),
        "loss_scale": jnp.clip(jnp.exp(jax.random.uniform(key_list[10], (), jnp.float32, math.log(2.0), math.log(8.0))), 2.0, 8.0),
    }


epsilon = 1e-06

def rms_parts(features):
    widened = features.astype(jnp.float32)
    inverse = lax.rsqrt(lax.optimization_barrier(jnp.mean(widened * widened, axis=1, keepdims=True)) + epsilon)
    return (widened * inverse, inverse)

def layer_forward(features, weight_in, weight_out):
    normed, inverse = rms_parts(features)
    preact = jnp.dot(normed.astype(jnp.bfloat16), weight_in, preferred_element_type=jnp.float32)
    hidden = jax.nn.gelu(preact).astype(jnp.bfloat16)
    blended = features.astype(jnp.float32) + jnp.dot(hidden, weight_out, preferred_element_type=jnp.float32)
    return (normed, inverse, preact, hidden, blended)

def block_sum(first_op, second_op, row_block):
    groups = first_op.shape[0] // row_block
    first_blocks = first_op.reshape(groups, row_block, first_op.shape[1])
    second_blocks = second_op.reshape(groups, row_block, second_op.shape[1])

    def accumulate(running, operands):
        partial_sum = jnp.dot(operands[0].T, operands[1], preferred_element_type=jnp.float32)
        rounded = lax.optimization_barrier(partial_sum.astype(jnp.bfloat16))
        return (running + rounded.astype(jnp.float32), None)
    start_sum = jnp.zeros((first_op.shape[1], second_op.shape[1]), jnp.float32)
    running, _ = lax.scan(accumulate, start_sum, (first_blocks, second_blocks))
    return running

def layer_backward(normed, inverse, preact, hidden, blended_grad, weight_in, weight_out, row_block):
    blended_b = blended_grad.astype(jnp.bfloat16)
    hidden_grad = jnp.dot(blended_b, weight_out.T, preferred_element_type=jnp.float32)
    _, pullback = jax.vjp(jax.nn.gelu, preact)
    preact_grad = pullback(hidden_grad)[0].astype(jnp.bfloat16)
    normed_grad = jnp.dot(preact_grad, weight_in.T, preferred_element_type=jnp.float32)
    average = lax.optimization_barrier(jnp.mean(normed * normed_grad, axis=1, keepdims=True))
    input_grad = blended_grad + (normed_grad - normed * average) * inverse
    grad_in = block_sum(normed.astype(jnp.bfloat16), preact_grad, row_block)
    grad_out = block_sum(hidden, blended_b, row_block)
    return (input_grad, grad_in, grad_out)

def reference(image_in, text_in, img_w1, img_w2, img_proj, txt_w1, txt_w2, label_offset, logit_scale, logit_bias, loss_scale):
    images = image_in[:N_TOWER - 1].reshape(BATCH, WI)
    texts = text_in[N_TOWER - 1]
    normed, inverse, preact, hidden, blended = layer_forward(images, img_w1, img_w2)
    blended_b = blended.astype(jnp.bfloat16)
    projected = jnp.dot(blended_b, img_proj, preferred_element_type=jnp.float32)
    length = jnp.sqrt(lax.optimization_barrier(jnp.sum(projected * projected, axis=1, keepdims=True)))
    embedded = (projected / length).astype(jnp.bfloat16)
    text_normed, text_inverse, text_preact, text_hidden, text_blended = layer_forward(texts, txt_w1, txt_w2)
    text_length = jnp.sqrt(lax.optimization_barrier(jnp.sum(text_blended * text_blended, axis=1, keepdims=True)))
    text_embed = (text_blended / text_length).astype(jnp.bfloat16)
    scores = jnp.dot(embedded, text_embed.T, preferred_element_type=jnp.float32)
    logits = logit_scale * scores + logit_bias
    row_ids = jnp.arange(BATCH, dtype=jnp.int32)
    offsets = label_offset[:N_TOWER - 1].reshape(-1)
    target = (row_ids + offsets[row_ids // ROW_DEV]) % BATCH
    positive = jnp.arange(BATCH, dtype=jnp.int32)[None, :] == target[:, None]
    signed = jnp.where(positive, jnp.float32(1.0), jnp.float32(-1.0))
    pair_grad = -loss_scale * signed * jax.nn.sigmoid(-signed * logits)
    pair_weight = (logit_scale * pair_grad).astype(jnp.bfloat16)
    embed_grad = jnp.dot(pair_weight, text_embed, preferred_element_type=jnp.float32)
    text_embed_grad = jnp.dot(pair_weight.T, embedded, preferred_element_type=jnp.float32)
    direction = projected / length
    proj_grad = ((embed_grad - direction * lax.optimization_barrier(jnp.sum(direction * embed_grad, axis=1, keepdims=True))) / length).astype(jnp.bfloat16)
    grad_proj = block_sum(blended_b, proj_grad, ROW_DEV)
    blended_grad = jnp.dot(proj_grad, img_proj.T, preferred_element_type=jnp.float32)
    image_dx, grad_w1, grad_w2 = layer_backward(normed, inverse, preact, hidden, blended_grad, img_w1, img_w2, ROW_DEV)
    text_direction = text_blended / text_length
    text_blended_grad = (text_embed_grad - text_direction * lax.optimization_barrier(jnp.sum(text_direction * text_embed_grad, axis=1, keepdims=True))) / text_length
    text_dx, grad_t1, grad_t2 = layer_backward(text_normed, text_inverse, text_preact, text_hidden, text_blended_grad, txt_w1, txt_w2, BATCH // N_DP)
    image_out = jnp.concatenate([image_dx.reshape(N_TOWER - 1, ROWS_SEC, WI), jnp.zeros((1, ROWS_SEC, WI), jnp.float32)], axis=0)
    text_out = jnp.concatenate([jnp.zeros((N_TOWER - 1, BATCH, WT), jnp.float32), text_dx[None]], axis=0)
    return (image_out, text_out, grad_w1, grad_w2, grad_proj, grad_t1, grad_t2)
```

```python
import functools
import math

import jax
import jax.numpy as jnp
from jax import lax
from jax.experimental import pallas as pl
from jax.experimental.pallas import tpu as pltpu
from jax.sharding import PartitionSpec as P

epsilon = 1e-06
bf16 = jnp.bfloat16
f32 = jnp.float32
MESH = pl.DeviceIdType.MESH
GELU_A = math.sqrt(2.0 / math.pi)
GELU_B = 0.044715

NT = 4
ND = 8
NM = 4
IR = 128
TR = 384
IQ = IR // NM
TQ = TR // NM
WI = 1792
WT = 1152
IS = WI // NM
TS = WT // NM
FI = 1920
FT = 640
BATCH = 3072
IO = WI // 32
TO = WT // 32
IP = 64
TP = 48
N_SEM = 320


def dot(a, b):
    return jnp.dot(a, b, preferred_element_type=f32)


def dot_t(a, b):
    return lax.dot_general(a, b, (((1,), (1,)), ((), ())), preferred_element_type=f32)


def dot_rows(a, b):
    return lax.dot_general(a, b, (((0,), (0,)), ((), ())), preferred_element_type=f32)


def gelu_both(u):
    sq = u * u
    th = jnp.tanh(GELU_A * u * (1.0 + GELU_B * sq))
    half = 0.5 * (1.0 + th)
    slope = half + 0.5 * u * (1.0 - th * th) * (GELU_A * (1.0 + 3.0 * GELU_B * sq))
    return u * half, slope


def scratch_list():
    v = pltpu.VMEM
    return dict(
        w1=v((WI, FI), bf16),
        w2=v((FI, WI), bf16),
        pj=v((NM, WI, TS), bf16),
        xs=v((NM, IR, IS), bf16),
        xt=v((NM, TR, TS), bf16),
        ns=v((NM, IR, IS), bf16),
        nt=v((NM, TR, TS), bf16),
        ivi=v((IR, 1), f32),
        ivt=v((TR, 1), f32),
        hi=v((3, IR, FI), bf16),
        ht=v((TR, FT), bf16),
        gi=v((IR, FI), f32),
        gt=v((TR, FT), f32),
        p2i=v((IR, WI), f32),
        p2t=v((TR, WT), f32),
        rc2i=v((2, IQ, WI), f32),
        rc2t=v((2, TQ, WT), f32),
        st2i=v((IQ, WI), bf16),
        st2t=v((TQ, WT), bf16),
        rx2i=v((IQ, WI), bf16),
        rx2t=v((TQ, WT), bf16),
        tb=v((TQ, WT), f32),
        tl=v((TQ, 1), f32),
        bl=v((NM, NM, IQ, IS), bf16),
        pr=v((IQ, WT), f32),
        ln=v((IQ, 1), f32),
        ei=v((NM, IQ, WT), bf16),
        et=v((NM, TQ, WT), bf16),
        cols=v((ND, TQ, WT), bf16),
        lab=v((ND, 3, 8, 128), f32),
        labo=v((8, 128), f32),
        q4t=v((TR, WT), f32),
        rc4t=v((2, TQ, WT), f32),
        st4t=v((TQ, WT), bf16),
        rx4t=v((TQ, WT), bf16),
        bfi=v((NM, IQ, WI), bf16),
        bft=v((NM, TQ, WT), bf16),
        pgs=v((NM, IQ, TS), bf16),
        pgr=v((NM, IQ, TS), bf16),
        bsi=v((NM, IR, IS), bf16),
        bst=v((NM, TR, TS), bf16),
        an=v((3, IR, IS), bf16),
        ant=v((TR, TS), bf16),
        ab=v((3, IR, IS), bf16),
        abt=v((TR, TS), bf16),
        al=v((3, NM, IQ, IS), bf16),
        bj=v((3, NM, IQ, TS), bf16),
        ki=v((3, IR, FI), bf16),
        kt=v((TR, FT), bf16),
        g6i=v((NM, IR, 512), f32),
        g6t=v((NM, TR, 384), f32),
        rc6i=v((2, IR, 512), f32),
        rc6t=v((2, TR, 384), f32),
        st6i=v((IR, 512), bf16),
        st6t=v((TR, 384), bf16),
        rx6i=v((IR, 512), bf16),
        rx6t=v((TR, 384), bf16),
        rb1=v((ND, IP, FI), bf16),
        sb2=v((ND, IP, FI), bf16),
        rb2=v((ND, IP, FI), bf16),
        sbj=v((ND, IP, TS), bf16),
        rbj=v((ND, IP, TS), bf16),
        sbt1=v((ND, TP, FT), bf16),
        rbt1=v((ND, TP, FT), bf16),
        sbt2=v((ND, TP, FT), bf16),
        rbt2=v((ND, TP, FT), bf16),
        sem=pltpu.SemaphoreType.DMA((N_SEM,)),
    )


NAMES = list(scratch_list())


def step_kernel(
    img_in, txt_in, w1_in, w2_in, pj_in, tw1_in, tw2_in, label, scale, bias, loss,
    o_img, o_txt, o_w1, o_w2, o_pj, o_t1, o_t2, *scratch
):
    r = dict(zip(NAMES, scratch))
    sem = r["sem"]
    used = [0]
    t = lax.axis_index("tower")
    d = lax.axis_index("dp")
    m = lax.axis_index("mp")
    core = m % 2
    high = m // 2
    ms = m + 1 - 2 * core
    mo = (m + 2) % NM
    md = (ms + 2) % NM
    text = t == NT - 1
    image = t != NT - 1
    ti = jnp.minimum(t, 2)
    sib, opp, diag = (t, d, ms), (t, d, mo), (t, d, md)
    others_t = [((t + k) % NT, d, m) for k in (1, 2, 3)]
    order_d = (4, 1, 3, 5, 7, 2, 6)
    others_d = [(d + k) % ND for k in order_d]

    def take(n):
        first = used[0]
        used[0] += n
        assert used[0] <= N_SEM
        return first

    img_sends, txt_sends, all_sends = [], [], []

    def send(src, dst, arrived, dev, group):
        copy = pltpu.make_async_remote_copy(
            src_ref=src, dst_ref=dst, send_sem=sem.at[take(1)], recv_sem=sem.at[arrived],
            device_id=dev, device_id_type=MESH,
        )
        group.append(copy)
        return copy

    def arrive(dst, arrived):
        pltpu.make_async_remote_copy(
            src_ref=dst, dst_ref=dst, send_sem=sem.at[0], recv_sem=sem.at[arrived],
            device_id=sib, device_id_type=MESH,
        ).wait_recv()

    def gather_mp(slot, group):
        b = take(NM)
        to_opp = send(slot(m), slot(m), b + m, opp, group)
        to_sib = send(slot(m), slot(m), b + m, sib, group)
        pass_on = send(slot(mo), slot(mo), b + mo, sib, group)

        def start():
            to_opp.start()
            to_sib.start()

        def middle():
            arrive(slot(mo), b + mo)
            pass_on.start()

        def finish():
            arrive(slot(ms), b + ms)
            arrive(slot(md), b + md)

        return start, middle, finish

    def sum_mp(quarter, rc, st, rx, group, pack=None):
        b = take(3)
        first, second = 1 - high, high
        s1 = send(quarter(2 * first + 1 - core), rc.at[first], b + first, sib, group)
        s2 = send(quarter(2 * second + 1 - core), rc.at[second], b + second, sib, group)
        cross = send(st, rx, b + 2, opp, group)

        def run():
            s1.start()
            s2.start()
            arrive(rc.at[first], b + first)
            part = quarter(2 * first + core)[...] + rc[first]
            st[...] = part.astype(bf16) if pack is None else pack(part)
            cross.start()
            arrive(rc.at[second], b + second)
            mine = quarter(2 * second + core)[...] + rc[second]
            arrive(rx, b + 2)
            return mine

        return run

    def exchange_x(src_img, dst_img, src_txt, dst_txt):
        b = take(NT)
        ci = [send(src_img(dev[0]), dst_img(ti), b + ti, dev, img_sends) for dev in others_t]
        ct = [send(src_txt(dev[0]), dst_txt, b + 3, dev, txt_sends) for dev in others_t] if src_txt else []

        def start_img():
            for c in ci:
                c.start()

        def start_txt():
            for c in ct:
                c.start()

        def finish():
            for s in range(3):
                @pl.when(t != s)
                def _(s=s):
                    arrive(dst_img(s), b + s)
            if src_txt:
                @pl.when(image)
                def _():
                    arrive(dst_txt, b + 3)

        return start_img, start_txt, finish

    def scatter_dp(sb, rb):
        b = take(ND)
        cs = [send(sb(dd), rb.at[d], b + d, (t, dd, m), all_sends) for dd in others_d]

        def start():
            for c in cs:
                c.start()

        def finish(rows):
            total = sb(d)[...].astype(f32)
            for dd in others_d:
                arrive(rb.at[dd], b + dd)
                total = total + rb[dd].astype(f32)
            return total[:rows]

        return start, finish

    lb = take(5)
    load_xi = pltpu.make_async_copy(img_in.at[0], r["xs"].at[m], sem.at[lb])
    load_xt = pltpu.make_async_copy(txt_in.at[0], r["xt"].at[m], sem.at[lb + 1])
    load_w1 = pltpu.make_async_copy(w1_in, r["w1"], sem.at[lb + 2])
    load_w2 = pltpu.make_async_copy(w2_in, r["w2"], sem.at[lb + 3])
    load_pj = pltpu.make_async_copy(pj_in, r["pj"].at[m], sem.at[lb + 4])
    tw1 = r["w1"].at[pl.ds(0, WT), pl.ds(0, FT)]
    tw2 = r["w2"].at[pl.ds(0, FT), pl.ds(0, WT)]
    load_t1 = pltpu.make_async_copy(tw1_in, tw1, sem.at[lb + 2])
    load_t2 = pltpu.make_async_copy(tw2_in, tw2, sem.at[lb + 3])

    xi_start, xi_mid, xi_fin = gather_mp(lambda i: r["xs"].at[i], img_sends)
    xt_start, xt_mid, xt_fin = gather_mp(lambda i: r["xt"].at[i], txt_sends)
    pj_start, pj_mid, pj_fin = gather_mp(lambda i: r["pj"].at[i], img_sends)

    lab_b = take(3)
    lab_up = send(r["labo"], r["lab"].at[d, ti], lab_b + ti, (NT - 1, d, m), img_sends)
    lab_d = take(ND)
    lab_out = [send(r["lab"].at[d], r["lab"].at[d], lab_d + d, (t, dd, m), txt_sends) for dd in others_d]

    sum2i = sum_mp(lambda q: r["p2i"].at[pl.ds(q * IQ, IQ)], r["rc2i"], r["st2i"], r["rx2i"], img_sends)
    sum2t = sum_mp(lambda q: r["p2t"].at[pl.ds(q * TQ, TQ)], r["rc2t"], r["st2t"], r["rx2t"], txt_sends)

    cols = r["cols"]
    star = take(3)
    star_img = send(r["ei"].at[m], cols.at[d, pl.ds(IQ * ti, IQ)], star + ti, (NT - 1, d, m), img_sends)
    star_txt = [
        send(r["et"].at[m, pl.ds(IQ * c, IQ)], cols.at[d, pl.ds(IQ * c, IQ)], star + c, dev, txt_sends)
        for c in range(3) for dev in others_t
    ]
    ring = take(3 * ND)
    ring_out = [
        [send(cols.at[d, pl.ds(IQ * c, IQ)], cols.at[d, pl.ds(IQ * c, IQ)], ring + ND * c + d, (t, dd, m), all_sends)
         for dd in others_d]
        for c in range(3)
    ]
    ei_start, ei_mid, ei_fin = gather_mp(lambda i: r["ei"].at[i], img_sends)
    et_start, et_mid, et_fin = gather_mp(lambda i: r["et"].at[i], txt_sends)
    bl_start, bl_mid, bl_fin = gather_mp(lambda i: r["bl"].at[i], img_sends)
    hid_si, hid_st, hid_fin = exchange_x(
        lambda s: r["hi"].at[ti], lambda s: r["hi"].at[s], lambda s: r["ht"], r["ht"])
    nor_si, nor_st, nor_fin = exchange_x(
        lambda s: r["ns"].at[s], lambda s: r["an"].at[s], lambda s: r["nt"].at[s], r["ant"])
    blx_si, _, blx_fin = exchange_x(
        lambda s: r["bl"].at[:, s], lambda s: r["al"].at[s], None, None)
    sum4i = sum_mp(lambda q: r["q4t"].at[pl.ds(q * IQ, IQ)], r["rc4t"].at[:, 0:IQ], r["st4t"].at[0:IQ], r["rx4t"].at[0:IQ], img_sends)
    sum4t = sum_mp(lambda q: r["q4t"].at[pl.ds(q * TQ, TQ)], r["rc4t"], r["st4t"], r["rx4t"], txt_sends)
    bi_start, bi_mid, bi_fin = gather_mp(lambda i: r["bfi"].at[i], img_sends)
    bt_start, bt_mid, bt_fin = gather_mp(lambda i: r["bft"].at[i], txt_sends)
    pgb = take(NM)
    pg_out = [
        send(r["pgs"].at[dev[2]], r["pgr"].at[m], pgb + m, dev, img_sends) for dev in (opp, diag, sib)
    ]
    pgx_si, _, pgx_fin = exchange_x(lambda s: r["pgr"], lambda s: r["bj"].at[s], None, None)
    bg_si, bg_st, bg_fin = exchange_x(
        lambda s: r["bsi"].at[s], lambda s: r["ab"].at[s], lambda s: r["bst"].at[s], r["abt"])
    pre_si, pre_st, pre_fin = exchange_x(
        lambda s: r["ki"].at[ti], lambda s: r["ki"].at[s], lambda s: r["kt"], r["kt"])

    def packer(width, full):
        def pack(part):
            rows = part.shape[0]
            tail = part[:, width:]
            lane = lax.broadcasted_iota(jnp.int32, (rows, full - width), 1)
            sums = jnp.sum(jnp.where(lane == 0, tail, 0.0), axis=1, keepdims=True)
            top = sums.astype(bf16).astype(f32)
            low = sums - top
            tail = jnp.where(lane == 0, top, jnp.where(lane == 1, low, 0.0))
            return jnp.concatenate([part[:, :width], tail], axis=1).astype(bf16)
        return pack

    sum6i = sum_mp(lambda q: r["g6i"].at[q], r["rc6i"], r["st6i"], r["rx6i"], img_sends, packer(IS, 512))
    sum6t = sum_mp(lambda q: r["g6t"].at[q], r["rc6t"], r["st6t"], r["rx6t"], txt_sends, packer(TS, 384))
    w2_start, w2_fin = scatter_dp(lambda i: r["sb2"].at[i], r["rb2"])
    t2_start, t2_fin = scatter_dp(lambda i: r["sbt2"].at[i], r["rbt2"])
    j_start, j_fin = scatter_dp(lambda i: r["sbj"].at[i], r["rbj"])
    w1_start, w1_fin = scatter_dp(lambda i: r["w1"].at[pl.ds(i * IP, IP)], r["rb1"])
    t1_start, t1_fin = scatter_dp(lambda i: r["sbt1"].at[i], r["rbt1"])

    @pl.when(image)
    def _():
        load_xi.start()
        load_w1.start()
        load_w2.start()
        load_pj.start()

    @pl.when(text)
    def _():
        load_xt.start()
        load_t1.start()
        load_t2.start()

    barrier = pltpu.get_barrier_semaphore()
    partners = [sib, opp, diag] + others_t + [(t, dd, m) for dd in others_d]
    for dev in partners:
        pl.semaphore_signal(barrier, inc=1, device_id=dev, device_id_type=MESH)
    pl.semaphore_wait(barrier, len(partners))

    @pl.when(image)
    def _():
        load_xi.wait()
        xi_start()
        r["labo"][...] = jnp.full((8, 128), label[0, 0].astype(f32))
        lab_up.start()
        load_pj.wait()
        pj_start()
        xi_mid()
        xi_fin()
        total = jnp.zeros((IR, 1), f32)
        for k in range(NM):
            x = r["xs"][k].astype(f32)
            total = total + jnp.sum(x * x, axis=1, keepdims=True)
        inv = lax.rsqrt(total / WI + epsilon)
        r["ivi"][...] = inv
        for k in range(NM):
            r["ns"][k] = (r["xs"][k].astype(f32) * inv).astype(bf16)
        load_w1.wait()

        def front(j, carry):
            at = pl.ds(pl.multiple_of(j * 384, 384), 384)
            u = dot(r["ns"][0], r["w1"][0:IS, at])
            for k in range(1, NM):
                u = u + dot(r["ns"][k], r["w1"][k * IS:(k + 1) * IS, at])
            val, slope = gelu_both(u)
            r["hi"][ti, :, at] = val.astype(bf16)
            r["gi"][:, at] = slope
            return carry

        lax.fori_loop(0, FI // 384, front, 0)
        load_w2.wait()

        def back(j, carry):
            at = pl.ds(pl.multiple_of(j * 256, 256), 256)
            r["p2i"][:, at] = dot(r["hi"][ti], r["w2"][:, at])
            return carry

        lax.fori_loop(0, WI // 256, back, 0)

    @pl.when(text)
    def _():
        load_xt.wait()
        xt_start()
        xt_mid()
        xt_fin()
        total = jnp.zeros((TR, 1), f32)
        for k in range(NM):
            x = r["xt"][k].astype(f32)
            total = total + jnp.sum(x * x, axis=1, keepdims=True)
        inv = lax.rsqrt(total / WT + epsilon)
        r["ivt"][...] = inv
        for k in range(NM):
            r["nt"][k] = (r["xt"][k].astype(f32) * inv).astype(bf16)
        load_t1.wait()

        def front(j, carry):
            at = pl.ds(pl.multiple_of(j * 128, 128), 128)
            u = dot(r["nt"][0], r["w1"][0:TS, at])
            for k in range(1, NM):
                u = u + dot(r["nt"][k], r["w1"][k * TS:(k + 1) * TS, at])
            val, slope = gelu_both(u)
            r["ht"][:, at] = val.astype(bf16)
            r["gt"][:, at] = slope
            return carry

        lax.fori_loop(0, FT // 128, front, 0)
        load_t2.wait()

        def back(j, carry):
            at = pl.ds(pl.multiple_of(j * 384, 384), 384)
            r["p2t"][:, at] = dot(r["ht"][...], r["w2"][0:FT, at])
            return carry

        lax.fori_loop(0, WT // 384, back, 0)
        for s in range(3):
            arrive(r["lab"].at[d, s], lab_b + s)
        for c in lab_out:
            c.start()

    @pl.when(image)
    def _():
        pj_mid()
        part = sum2i()
        rows = pl.ds(pl.multiple_of(m * IQ, IQ), IQ)
        x = jnp.concatenate([r["xs"][k, rows, :].astype(f32) for k in range(NM)], axis=1)
        blended = (x + (part + r["rx2i"][...].astype(f32))).astype(bf16)
        for k in range(NM):
            r["bl"][m, k] = blended[:, k * IS:(k + 1) * IS]
        pj_fin()
        projected = jnp.concatenate([dot(blended, r["pj"][k]) for k in range(NM)], axis=1)
        length = jnp.sqrt(jnp.sum(projected * projected, axis=1, keepdims=True))
        r["pr"][...] = projected
        r["ln"][...] = length
        r["ei"][m] = (projected / length).astype(bf16)
        star_img.start()
        ei_start()
        bl_start()

    @pl.when(text)
    def _():
        part = sum2t()
        rows = pl.ds(pl.multiple_of(m * TQ, TQ), TQ)
        x = jnp.concatenate([r["xt"][k, rows, :].astype(f32) for k in range(NM)], axis=1)
        blended = x + (part + r["rx2t"][...].astype(f32))
        length = jnp.sqrt(jnp.sum(blended * blended, axis=1, keepdims=True))
        r["tb"][...] = blended
        r["tl"][...] = length
        r["et"][m] = (blended / length).astype(bf16)
        for c in star_txt:
            c.start()
        et_start()

    for c in range(3):
        arrive(cols.at[d, pl.ds(IQ * c, IQ)], star + c)
        for copy in ring_out[c]:
            copy.start()

    @pl.when(image)
    def _():
        ei_mid()
        hid_si()
        nor_si()
        bl_mid()
        ei_fin()

    @pl.when(text)
    def _():
        et_mid()
        hid_st()
        nor_st()
        et_fin()
        for dd in others_d:
            arrive(r["lab"].at[dd], lab_d + dd)

    scale_v, bias_v, loss_v = scale[0, 0], bias[0, 0], loss[0, 0]

    def weight(scores, positive):
        logits = scale_v * scores + bias_v
        signed = jnp.where(positive, 1.0, -1.0).astype(f32)
        grad = -loss_v * signed * jax.nn.sigmoid(-signed * logits)
        return (scale_v * grad).astype(bf16)

    def block_ready(dd):
        for c in range(3):
            arrive(cols.at[dd, pl.ds(IQ * c, IQ)], ring + ND * c + dd)

    @pl.when(image)
    def _():
        emb = r["ei"][...].reshape(IR, WT)
        row = (t * ND + d) * IR + lax.broadcasted_iota(jnp.int32, (IR, TQ), 0) + label[0, 0]
        target = jnp.where(row >= BATCH, row - BATCH, row)
        lane = lax.broadcasted_iota(jnp.int32, (IR, TQ), 1)

        def block(dd):
            pw = weight(dot_t(emb, cols[dd]), target == lane + (dd * TR + m * TQ))
            return dot(pw, cols[dd])

        r["q4t"][0:IR] = block(d)

        def step(k, carry):
            dd = (d + k) % ND
            block_ready(dd)
            r["q4t"][0:IR] += block(dd)
            return carry

        lax.fori_loop(1, ND, step, 0)

    @pl.when(text)
    def _():
        emb = r["et"][...].reshape(TR, WT)
        row = d * TR + lax.broadcasted_iota(jnp.int32, (TR, TQ), 0)
        lane = lax.broadcasted_iota(jnp.int32, (1, TQ), 1)
        part = lane // IQ

        def block(dd):
            off = r["lab"][dd]
            off = jnp.where(part == 0, off[0, :1, :TQ], jnp.where(part == 1, off[1, :1, :TQ], off[2, :1, :TQ]))
            own = (part * ND + dd) * IR + m * IQ + lane % IQ
            target = own + off.astype(jnp.int32)
            target = jnp.where(target >= BATCH, target - BATCH, target)
            pw = weight(dot_t(emb, cols[dd]), row == target)
            return dot(pw, cols[dd])

        r["q4t"][...] = block(d)

        def step(k, carry):
            dd = (d + k) % ND
            block_ready(dd)
            r["q4t"][...] += block(dd)
            return carry

        lax.fori_loop(1, ND, step, 0)

    @pl.when(image)
    def _():
        part = sum4i()
        grad = part + r["rx4t"][0:IQ].astype(f32)
        length = r["ln"][...]
        direction = r["pr"][...] / length
        pg = ((grad - direction * jnp.sum(direction * grad, axis=1, keepdims=True)) / length).astype(bf16)
        blended_grad = jnp.zeros((IQ, WI), f32)
        for k in range(NM):
            piece = pg[:, k * TS:(k + 1) * TS]
            r["pgs"][k] = piece
            blended_grad = blended_grad + dot_t(piece, r["pj"][k])
        r["bfi"][m] = blended_grad.astype(bf16)
        bi_start()
        r["pgr"][m] = r["pgs"][m]
        for c in pg_out:
            c.start()
        bl_fin()
        blx_si()
        r["al"][ti] = r["bl"][:, ti]
        r["an"][ti] = r["ns"][ti]
        bi_mid()
        bi_fin()
        grads = r["bfi"][...].reshape(IR, WI)
        for k in range(NM):
            r["bsi"][k] = grads[:, k * IS:(k + 1) * IS]
        bg_si()
        r["ab"][ti] = r["bsi"][ti]

        def front(j, carry):
            at = pl.ds(pl.multiple_of(j * 384, 384), 384)
            hg = dot_t(r["bfi"][...].reshape(IR, WI), r["w2"][at, :])
            r["ki"][ti, :, at] = (hg * r["gi"][:, at]).astype(bf16)
            return carry

        lax.fori_loop(0, FI // 384, front, 0)
        pre_si()
        for dev in (opp, diag, sib):
            arrive(r["pgr"].at[dev[2]], pgb + dev[2])
        pgx_si()
        r["bj"][ti] = r["pgr"][...]

    @pl.when(text)
    def _():
        part = sum4t()
        grad = part + r["rx4t"][...].astype(f32)
        length = r["tl"][...]
        direction = r["tb"][...] / length
        blended_grad = (grad - direction * jnp.sum(direction * grad, axis=1, keepdims=True)) / length
        r["bft"][m] = blended_grad.astype(bf16)
        bt_start()
        r["ant"][...] = r["nt"][NT - 1]
        bt_mid()
        bt_fin()
        grads = r["bft"][...].reshape(TR, WT)
        for k in range(NM):
            r["bst"][k] = grads[:, k * TS:(k + 1) * TS]
        bg_st()
        r["abt"][...] = r["bst"][NT - 1]

        def front(j, carry):
            at = pl.ds(pl.multiple_of(j * 128, 128), 128)
            hg = dot_t(r["bft"][...].reshape(TR, WT), r["w2"][at, 0:WT])
            r["kt"][:, at] = (hg * r["gt"][:, at]).astype(bf16)
            return carry

        lax.fori_loop(0, FT // 128, front, 0)
        pre_st()

    def product(a, b_ref, sb, rows, padded, width, lead):
        def tile(j, carry):
            at = pl.ds(pl.multiple_of(j * width, width), width)
            b = b_ref[:, :, at].reshape(lead, width) if len(b_ref.shape) == 3 else b_ref[:, at]
            g = dot_rows(a, b)
            pad = jnp.zeros((padded - rows, width), f32)
            for dd in range(ND):
                piece = jnp.concatenate([g[dd * rows:(dd + 1) * rows], pad], axis=0)
                sb(dd)[:, at] = piece.astype(bf16)
            return carry

        lax.fori_loop(0, b_ref.shape[-1] // width, tile, 0)

    hid_fin()
    bg_fin()
    product(r["ab"][...].reshape(3 * IR, IS), r["hi"], lambda i: r["sb2"].at[i], IO, IP, 384, 3 * IR)
    w2_start()
    product(r["abt"][...], r["ht"], lambda i: r["sbt2"].at[i], TO, TP, 128, TR)
    t2_start()

    @pl.when(image)
    def _():
        total = jnp.zeros((IR, 1), f32)
        inv = r["ivi"][...]
        lane = lax.broadcasted_iota(jnp.int32, (IR, 512 - IS), 1)
        for k in range(NM):
            g = dot_t(r["ki"][ti], r["w1"][k * IS:(k + 1) * IS, :])
            total = total + jnp.sum(r["xs"][k].astype(f32) * inv * g, axis=1, keepdims=True)
            r["g6i"][k, :, 0:IS] = g
        tail = jnp.where(lane == 0, total, 0.0)
        for k in range(NM):
            r["g6i"][k, :, IS:512] = tail
        part = sum6i()
        other = r["rx6i"][...].astype(f32)
        sums = part[:, IS:] + other[:, IS:]
        sums = jnp.where(lane == 0, sums, jnp.where(lane == 1, other[:, IS:], 0.0))
        average = jnp.sum(sums, axis=1, keepdims=True) / WI
        grad = part[:, :IS] + other[:, :IS]
        normed = r["xs"][m].astype(f32) * inv
        o_img[0] = r["bsi"][m].astype(f32) + (grad - normed * average) * inv
        o_txt[0] = jnp.zeros((TR, TS), f32)

    @pl.when(text)
    def _():
        total = jnp.zeros((TR, 1), f32)
        inv = r["ivt"][...]
        lane = lax.broadcasted_iota(jnp.int32, (TR, 384 - TS), 1)
        for k in range(NM):
            g = dot_t(r["kt"][...], r["w1"][k * TS:(k + 1) * TS, 0:FT])
            total = total + jnp.sum(r["xt"][k].astype(f32) * inv * g, axis=1, keepdims=True)
            r["g6t"][k, :, 0:TS] = g
        tail = jnp.where(lane == 0, total, 0.0)
        for k in range(NM):
            r["g6t"][k, :, TS:384] = tail
        part = sum6t()
        other = r["rx6t"][...].astype(f32)
        sums = part[:, TS:] + other[:, TS:]
        sums = jnp.where(lane == 0, sums, jnp.where(lane == 1, other[:, TS:], 0.0))
        average = jnp.sum(sums, axis=1, keepdims=True) / WT
        grad = part[:, :TS] + other[:, :TS]
        normed = r["xt"][m].astype(f32) * inv
        o_txt[0] = r["bst"][m].astype(f32) + (grad - normed * average) * inv
        o_img[0] = jnp.zeros((IR, IS), f32)

    blx_fin()
    pgx_fin()
    b = r["bj"][...].reshape(3 * IR, TS)
    g = dot_rows(r["al"][...].reshape(3 * IR, IS), b)
    pad = jnp.zeros((IP - IO, TS), f32)
    for dd in range(ND):
        r["sbj"][dd] = jnp.concatenate([g[dd * IO:(dd + 1) * IO], pad], axis=0).astype(bf16)
    j_start()
    nor_fin()
    pre_fin()
    product(r["an"][...].reshape(3 * IR, IS), r["ki"], lambda i: r["w1"].at[pl.ds(i * IP, IP)], IO, IP, 384, 3 * IR)
    w1_start()
    product(r["ant"][...], r["kt"], lambda i: r["sbt1"].at[i], TO, TP, 128, TR)
    t1_start()

    o_w2[...] = w2_fin(IO)
    o_t2[...] = t2_fin(TO)
    o_pj[...] = j_fin(IO)
    o_w1[...] = w1_fin(IO)
    o_t1[...] = t1_fin(TO)

    for c in all_sends:
        c.wait_send()

    @pl.when(image)
    def _():
        for c in img_sends:
            c.wait_send()

    @pl.when(text)
    def _():
        for c in txt_sends:
            c.wait_send()


def per_device(
    image_in, text_in, img_w1, img_w2, img_proj, txt_w1, txt_w2, label_offset,
    logit_scale, logit_bias, loss_scale,
):
    anywhere = pl.BlockSpec(memory_space=pl.ANY)
    scalar = pl.BlockSpec(memory_space=pltpu.SMEM)
    vmem = pl.BlockSpec(memory_space=pltpu.VMEM)
    one = lambda v: v.reshape(1, 1)
    outs = pl.pallas_call(
        step_kernel,
        out_shape=[
            jax.ShapeDtypeStruct((1, IR, IS), f32),
            jax.ShapeDtypeStruct((1, TR, TS), f32),
            jax.ShapeDtypeStruct((IO, FI), f32),
            jax.ShapeDtypeStruct((IO, FI), f32),
            jax.ShapeDtypeStruct((IO, TS), f32),
            jax.ShapeDtypeStruct((TO, FT), f32),
            jax.ShapeDtypeStruct((TO, FT), f32),
        ],
        in_specs=[anywhere] * 7 + [scalar] * 4,
        out_specs=[vmem] * 7,
        scratch_shapes=list(scratch_list().values()),
        compiler_params=pltpu.CompilerParams(
            collective_id=0, has_side_effects=True, vmem_limit_bytes=63 << 20
        ),
        name="step",
    )(
        image_in, text_in, img_w1, img_w2, img_proj, txt_w1, txt_w2, label_offset,
        one(logit_scale), one(logit_bias), one(loss_scale),
    )
    g_img, g_txt, g_w1, g_w2, g_pj, g_t1, g_t2 = outs
    return (g_img, g_txt, g_w1, g_w2.T, g_pj, g_t1, g_t2.T)


def solution(mesh):
    return jax.shard_map(
        per_device,
        mesh=mesh,
        in_specs=(
            P("tower", "dp", "mp"),
            P("tower", "dp", "mp"),
            P(None, "mp"),
            P("mp", None),
            P(None, "mp"),
            P(None, "mp"),
            P("mp", None),
            P("tower", "dp"),
            P(),
            P(),
            P(),
        ),
        out_specs=(
            P("tower", "dp", "mp"),
            P("tower", "dp", "mp"),
            P(("tower", "dp"), "mp"),
            P("mp", ("tower", "dp")),
            P(("tower", "dp"), "mp"),
            P(("tower", "dp"), "mp"),
            P("mp", ("tower", "dp")),
        ),
        check_vma=False,
    )
```

```python
import functools
import math

import jax
import jax.numpy as jnp
from jax import lax
from jax.experimental import pallas as pl
from jax.experimental.pallas import tpu as pltpu
from jax.sharding import PartitionSpec as P

epsilon = 1e-06
bf16 = jnp.bfloat16
f32 = jnp.float32
MESH = pl.DeviceIdType.MESH
GELU_A = math.sqrt(2.0 / math.pi)
GELU_B = 0.044715

NT = 4
ND = 8
NM = 4
IR = 128
TR = 384
IQ = IR // NM
TQ = TR // NM
WI = 1792
WT = 1152
IS = WI // NM
TS = WT // NM
FI = 1920
FT = 640
BATCH = 3072
IO = WI // 32
TO = WT // 32
IP = 64
TP = 48
IG = IS + 16
TG = TS + 16
FC = 640
N_SEM = 420
LIMIT = None


def dot(a, b):
    return jnp.dot(a, b, preferred_element_type=f32)


def dot_t(a, b):
    return lax.dot_general(a, b, (((1,), (1,)), ((), ())), preferred_element_type=f32)


def dot_rows(a, b):
    return lax.dot_general(a, b, (((0,), (0,)), ((), ())), preferred_element_type=f32)


def gelu_both(u):
    sq = u * u
    th = jnp.tanh(GELU_A * u * (1.0 + GELU_B * sq))
    half = 0.5 * (1.0 + th)
    slope = half + 0.5 * u * (1.0 - th * th) * (GELU_A * (1.0 + 3.0 * GELU_B * sq))
    return u * half, slope


def scratch_list():
    v = pltpu.VMEM
    return dict(
        w1=v((WI, FI), bf16),
        w2=v((FI, WI), bf16),
        pj=v((WT, WI), bf16),
        xs=v((WI, IR), bf16),
        xt=v((WT, TR), bf16),
        xf=v((IR, WI), bf16),
        xtf=v((TR, WT), bf16),
        ns=v((WI, IR), bf16),
        nt=v((WT, TR), bf16),
        nf=v((IR, WI), bf16),
        ntf=v((TR, WT), bf16),
        ivi=v((1, IR), f32),
        ivt=v((1, TR), f32),
        hi=v((3, IR, FI), bf16),
        ht=v((TR, FT), bf16),
        gi=v((IR, FI), f32),
        gt=v((TR, FT), f32),
        p2i=v((IR, WI), f32),
        p2t=v((TR, WT), f32),
        rc2i=v((2, IQ, WI), f32),
        rc2t=v((2, TQ, WT), f32),
        st2i=v((IQ, WI), bf16),
        st2t=v((TQ, WT), bf16),
        rx2i=v((IQ, WI), bf16),
        rx2t=v((TQ, WT), bf16),
        tb=v((TQ, WT), f32),
        tl=v((TQ, 1), f32),
        bl=v((NM, NM, IQ, IS), bf16),
        pr=v((IQ, WT), f32),
        ln=v((IQ, 1), f32),
        ei=v((NM, IQ, WT), bf16),
        et=v((NM, TQ, WT), bf16),
        cols=v((ND, TQ, WT), bf16),
        lab=v((ND, 3, 8, 128), f32),
        labo=v((8, 128), f32),
        q4t=v((TR, WT), f32),
        rc4t=v((2, TQ, WT), f32),
        st4t=v((TQ, WT), bf16),
        rx4t=v((TQ, WT), bf16),
        bfi=v((NM, IQ, WI), bf16),
        bft=v((NM, TQ, WT), bf16),
        pgf=v((IQ, WT), bf16),
        pgs=v((NM, IQ, TS), bf16),
        pgr=v((NM, IQ, TS), bf16),
        bsi=v((WI, IR), bf16),
        bst=v((WT, TR), bf16),
        an=v((3, IS, IR), bf16),
        ant=v((TS, TR), bf16),
        ab=v((3, IS, IR), bf16),
        abt=v((TS, TR), bf16),
        al=v((3, NM, IQ, IS), bf16),
        bj=v((3, NM, IQ, TS), bf16),
        ki=v((3, IR, FI), bf16),
        kt=v((TR, FT), bf16),
        g6i=v((NM, IG, IR), f32),
        g6t=v((NM, TG, TR), f32),
        rc6i=v((2, IG, IR), f32),
        rc6t=v((2, TG, TR), f32),
        st6i=v((IG, IR), bf16),
        st6t=v((TG, TR), bf16),
        rx6i=v((IG, IR), bf16),
        rx6t=v((TG, TR), bf16),
        ra1=v((2, 4 * IO, FI), bf16),
        sc1=v((4, IP, FI), bf16),
        rc1=v((4, IP, FI), bf16),
        ra2=v((4, 2 * IO, FI), bf16),
        sc2=v((2, IP, FI), bf16),
        rc2=v((2, IP, FI), bf16),
        sbj=v((2, 4 * IO, TS), bf16),
        raj=v((2, 4 * IO, TS), bf16),
        scj=v((4, IP, TS), bf16),
        rcj=v((4, IP, TS), bf16),
        sbt1=v((4, 2 * TO, FT), bf16),
        rat1=v((4, 2 * TO, FT), bf16),
        sct1=v((2, TP, FT), bf16),
        rct1=v((2, TP, FT), bf16),
        sbt2=v((2, 4 * TO, FT), bf16),
        rat2=v((2, 4 * TO, FT), bf16),
        sct2=v((4, TP, FT), bf16),
        rct2=v((4, TP, FT), bf16),
        sem=pltpu.SemaphoreType.DMA((N_SEM,)),
    )


NAMES = list(scratch_list())


def step_kernel(
    img_in, txt_in, w1_in, w2_in, pj_in, tw1_in, tw2_in, label, scale, bias, loss,
    o_img, o_txt, o_w1, o_w2, o_pj, o_t1, o_t2, *scratch
):
    r = dict(zip(NAMES, scratch))
    sem = r["sem"]
    used = [0]
    t = lax.axis_index("tower")
    d = lax.axis_index("dp")
    m = lax.axis_index("mp")
    core = m % 2
    high = m // 2
    ms = m + 1 - 2 * core
    mo = (m + 2) % NM
    md = (ms + 2) % NM
    text = t == NT - 1
    image = t != NT - 1
    ti = jnp.minimum(t, 2)
    sib, opp, diag = (t, d, ms), (t, d, mo), (t, d, md)
    dy = d // 4
    dz = d % 4
    others_t = [((t + k) % NT, d, m) for k in (1, 2, 3)]
    order_d = (4, 1, 3, 5, 7, 2, 6)
    others_d = [(d + k) % ND for k in order_d]

    def take(n):
        first = used[0]
        used[0] += n
        assert used[0] <= N_SEM
        return first

    img_sends, txt_sends, all_sends = [], [], []
    plans = []

    class Tracked:
        def __init__(self, copy, group):
            self.copy, self.group = copy, group

        def start(self):
            self.copy.start()
            self.group.append(self.copy)

    def plan(group, *steps):
        entry = {"group": group, "left": list(steps), "begun": False}
        plans.append(entry)

        def runner(step):
            def run(*args):
                entry["begun"] = True
                entry["left"].remove(step)
                return step(*args)
            return run

        return [runner(s) for s in steps]

    def send(src, dst, arrived, dev, group):
        copy = pltpu.make_async_remote_copy(
            src_ref=src, dst_ref=dst, send_sem=sem.at[take(1)], recv_sem=sem.at[arrived],
            device_id=dev, device_id_type=MESH,
        )
        return Tracked(copy, group)

    def arrive(dst, arrived):
        pltpu.make_async_remote_copy(
            src_ref=dst, dst_ref=dst, send_sem=sem.at[0], recv_sem=sem.at[arrived],
            device_id=sib, device_id_type=MESH,
        ).wait_recv()

    def gather_mp(slot, group):
        b = take(NM)
        to_opp = send(slot(m), slot(m), b + m, opp, group)
        to_sib = send(slot(m), slot(m), b + m, sib, group)
        pass_on = send(slot(mo), slot(mo), b + mo, sib, group)

        def start():
            to_opp.start()
            to_sib.start()

        def middle():
            arrive(slot(mo), b + mo)
            pass_on.start()

        def finish():
            arrive(slot(ms), b + ms)
            arrive(slot(md), b + md)

        return plan(group, start, middle, finish)

    def sum_mp(quarter, rc, st, rx, group, pack=None):
        b = take(3)
        first, second = 1 - high, high
        s1 = send(quarter(2 * first + 1 - core), rc.at[first], b + first, sib, group)
        s2 = send(quarter(2 * second + 1 - core), rc.at[second], b + second, sib, group)
        cross = send(st, rx, b + 2, opp, group)

        def start():
            s1.start()
            s2.start()

        def middle():
            arrive(rc.at[first], b + first)
            part = quarter(2 * first + core)[...] + rc[first]
            st[...] = part.astype(bf16) if pack is None else pack(part)
            cross.start()

        def finish():
            arrive(rc.at[second], b + second)
            mine = quarter(2 * second + core)[...] + rc[second]
            arrive(rx, b + 2)
            return mine

        return plan(group, start, middle, finish)

    def exchange_x(src_img, dst_img, src_txt, dst_txt):
        b = take(NT)
        ci = [send(src_img(dev[0]), dst_img(ti), b + ti, dev, img_sends) for dev in others_t]
        ct = [send(src_txt(dev[0]), dst_txt, b + 3, dev, txt_sends) for dev in others_t] if src_txt else []

        def start_img():
            for c in ci:
                c.start()

        def start_txt():
            for c in ct:
                c.start()

        def finish():
            for s in range(3):
                @pl.when(t != s)
                def _(s=s):
                    arrive(dst_img(s), b + s)
            if src_txt:
                @pl.when(image)
                def _():
                    arrive(dst_txt, b + 3)

        return plan(all_sends, start_img, start_txt, finish)

    def scatter_dp(mode, own, padded, spans, first, first_in, second, second_in):
        along_y = mode == "y"
        parts = 2 if along_y else 4
        me, rest = (dy, dz) if along_y else (dz, dy)

        def dev_first(p):
            return (t, p * 4 + dz, m) if along_y else (t, dy * 4 + p, m)

        def dev_second(p):
            return (t, dy * 4 + p, m) if along_y else (t, p * 4 + dz, m)

        steps = []
        for j, span in enumerate(spans):
            b1, b2 = take(4), take(4)
            one = [(me + k) % parts for k in range(1, parts)]
            two = [(rest + k) % (8 // parts) for k in range(1, 8 // parts)]
            c1 = [send(first(j, p), first_in.at[me, :, span], b1 + me, dev_first(p), all_sends) for p in one]
            c2 = [send(second.at[p, :, span], second_in.at[rest, :, span], b2 + rest, dev_second(p), all_sends)
                  for p in two]

            def start(c1=c1):
                for c in c1:
                    c.start()

            def middle(j=j, span=span, one=one, b1=b1, c2=c2):
                total = first(j, me)[...].astype(f32)
                for p in one:
                    arrive(first_in.at[p, :, span], b1 + p)
                    total = total + first_in[p, :, span].astype(f32)
                pad = jnp.zeros((padded - own, total.shape[1]), f32)
                for k in range(8 // parts):
                    piece = jnp.concatenate([total[k * own:(k + 1) * own], pad], axis=0)
                    second[k, :, span] = piece.astype(bf16)
                for c in c2:
                    c.start()

            def finish(out=None, span=span, two=two, b2=b2):
                total = second[rest, :, span].astype(f32)
                for p in two:
                    arrive(second_in.at[p, :, span], b2 + p)
                    total = total + second_in[p, :, span].astype(f32)
                if out is not None:
                    out[:, span] = total[:own]

            steps.append(plan(all_sends, start, middle, finish))
        return steps

    lb = take(5)
    mi = pl.ds(pl.multiple_of(m * IS, IS), IS)
    mt = pl.ds(pl.multiple_of(m * TS, TS), TS)
    load_xi = pltpu.make_async_copy(img_in.at[0], r["xs"].at[mi], sem.at[lb])
    load_xt = pltpu.make_async_copy(txt_in.at[0], r["xt"].at[mt], sem.at[lb + 1])
    load_w1 = pltpu.make_async_copy(w1_in, r["w1"], sem.at[lb + 2])
    load_w2 = pltpu.make_async_copy(w2_in, r["w2"], sem.at[lb + 3])
    load_pj = pltpu.make_async_copy(pj_in, r["pj"].at[mt], sem.at[lb + 4])
    tw1 = r["w1"].at[pl.ds(0, WT), pl.ds(0, FT)]
    tw2 = r["w2"].at[pl.ds(0, FT), pl.ds(0, WT)]
    load_t1 = pltpu.make_async_copy(tw1_in, tw1, sem.at[lb + 2])
    load_t2 = pltpu.make_async_copy(tw2_in, tw2, sem.at[lb + 3])

    xi_start, xi_mid, xi_fin = gather_mp(lambda i: r["xs"].at[pl.ds(pl.multiple_of(i * IS, IS), IS)], img_sends)
    xt_start, xt_mid, xt_fin = gather_mp(lambda i: r["xt"].at[pl.ds(pl.multiple_of(i * TS, TS), TS)], txt_sends)
    pj_start, pj_mid, pj_fin = gather_mp(lambda i: r["pj"].at[pl.ds(pl.multiple_of(i * TS, TS), TS)], img_sends)

    lab_b = take(3)
    lab_up = send(r["labo"], r["lab"].at[d, ti], lab_b + ti, (NT - 1, d, m), img_sends)
    lab_d = take(ND)
    lab_out = [send(r["lab"].at[d], r["lab"].at[d], lab_d + d, (t, dd, m), txt_sends) for dd in others_d]

    s2i_start, s2i_mid, s2i_fin = sum_mp(lambda q: r["p2i"].at[pl.ds(q * IQ, IQ)], r["rc2i"], r["st2i"], r["rx2i"], img_sends)
    s2t_start, s2t_mid, s2t_fin = sum_mp(lambda q: r["p2t"].at[pl.ds(q * TQ, TQ)], r["rc2t"], r["st2t"], r["rx2t"], txt_sends)

    cols = r["cols"]
    star = take(3)
    star_img = send(r["ei"].at[m], cols.at[d, pl.ds(IQ * ti, IQ)], star + ti, (NT - 1, d, m), img_sends)
    star_txt = [
        send(r["et"].at[m, pl.ds(IQ * c, IQ)], cols.at[d, pl.ds(IQ * c, IQ)], star + c, dev, txt_sends)
        for c in range(3) for dev in others_t
    ]
    ring = take(3 * ND)
    ring_out = [
        [send(cols.at[d, pl.ds(IQ * c, IQ)], cols.at[d, pl.ds(IQ * c, IQ)], ring + ND * c + d, (t, dd, m), all_sends)
         for dd in others_d]
        for c in range(3)
    ]
    ei_start, ei_mid, ei_fin = gather_mp(lambda i: r["ei"].at[i], img_sends)
    et_start, et_mid, et_fin = gather_mp(lambda i: r["et"].at[i], txt_sends)
    bl_start, bl_mid, bl_fin = gather_mp(lambda i: r["bl"].at[i], img_sends)
    hid_si, hid_st, hid_fin = exchange_x(
        lambda s: r["hi"].at[ti], lambda s: r["hi"].at[s], lambda s: r["ht"], r["ht"])
    nor_si, nor_st, nor_fin = exchange_x(
        lambda s: r["ns"].at[pl.ds(s * IS, IS)], lambda s: r["an"].at[s], lambda s: r["nt"].at[pl.ds(s * TS, TS)], r["ant"])
    blx_si, _, blx_fin = exchange_x(
        lambda s: r["bl"].at[:, s], lambda s: r["al"].at[s], None, None)
    s4i_start, s4i_mid, s4i_fin = sum_mp(lambda q: r["q4t"].at[pl.ds(q * IQ, IQ)], r["rc4t"].at[:, 0:IQ], r["st4t"].at[0:IQ], r["rx4t"].at[0:IQ], img_sends)
    s4t_start, s4t_mid, s4t_fin = sum_mp(lambda q: r["q4t"].at[pl.ds(q * TQ, TQ)], r["rc4t"], r["st4t"], r["rx4t"], txt_sends)
    bi_start, bi_mid, bi_fin = gather_mp(lambda i: r["bfi"].at[i], img_sends)
    bt_start, bt_mid, bt_fin = gather_mp(lambda i: r["bft"].at[i], txt_sends)
    pgb = take(NM)
    pg_out = [
        send(r["pgs"].at[dev[2]], r["pgr"].at[m], pgb + m, dev, img_sends) for dev in (opp, diag, sib)
    ]
    pgx_si, _, pgx_fin = exchange_x(lambda s: r["pgr"], lambda s: r["bj"].at[s], None, None)
    bg_si, bg_st, bg_fin = exchange_x(
        lambda s: r["bsi"].at[pl.ds(s * IS, IS)], lambda s: r["ab"].at[s], lambda s: r["bst"].at[pl.ds(s * TS, TS)], r["abt"])
    pre = []
    for j in range(FI // FC):
        at = slice(j * FC, (j + 1) * FC)
        pre.append(exchange_x(
            lambda s, at=at: r["ki"].at[ti, :, at], lambda s, at=at: r["ki"].at[s, :, at],
            (lambda s: r["kt"]) if j == 0 else None, r["kt"]))

    def packer(width):
        def pack(part):
            sums = part[width:]
            top = sums.astype(bf16).astype(f32)
            at = lax.broadcasted_iota(jnp.int32, sums.shape, 0)
            tail = jnp.where(at == 1, sums[0:1] - top[0:1], top)
            return jnp.concatenate([part[:width], tail], axis=0).astype(bf16)
        return pack

    s6i_start, s6i_mid, s6i_fin = sum_mp(lambda q: r["g6i"].at[q], r["rc6i"], r["st6i"], r["rx6i"], img_sends, packer(IS))
    s6t_start, s6t_mid, s6t_fin = sum_mp(lambda q: r["g6t"].at[q], r["rc6t"], r["st6t"], r["rx6t"], txt_sends, packer(TS))
    spans = [slice(j * FC, (j + 1) * FC) for j in range(FI // FC)]
    whole_t = [slice(0, FT)]
    whole_j = [slice(0, TS)]
    def sb2(j, p):
        return r["w2"].at[pl.ds(pl.multiple_of(j * 8 * IO + p * 2 * IO, 2 * IO), 2 * IO), 0:FC]

    def sb1(j, p):
        return r["w1"].at[pl.ds(pl.multiple_of(p * 4 * IO, 4 * IO), 4 * IO), spans[j]]

    w2_steps = scatter_dp(
        "z", IO, IP, spans, sb2, r["ra2"], r["sc2"], r["rc2"])
    w1_steps = scatter_dp(
        "y", IO, IP, spans, sb1, r["ra1"], r["sc1"], r["rc1"])
    t2_steps = scatter_dp("y", TO, TP, whole_t, lambda j, p: r["sbt2"].at[p], r["rat2"], r["sct2"], r["rct2"])
    t1_steps = scatter_dp("z", TO, TP, whole_t, lambda j, p: r["sbt1"].at[p], r["rat1"], r["sct1"], r["rct1"])
    pj_steps = scatter_dp("y", IO, IP, whole_j, lambda j, p: r["sbj"].at[p], r["raj"], r["scj"], r["rcj"])

    @pl.when(image)
    def _():
        load_xi.start()
        load_w1.start()
        load_w2.start()
        load_pj.start()

    @pl.when(text)
    def _():
        load_xt.start()
        load_t1.start()
        load_t2.start()

    barrier = pltpu.get_barrier_semaphore()
    partners = [sib, opp, diag] + others_t + [(t, dd, m) for dd in others_d]
    for dev in partners:
        pl.semaphore_signal(barrier, inc=1, device_id=dev, device_id_type=MESH)
    pl.semaphore_wait(barrier, len(partners))

    @pl.when(image)
    def _():
        load_xi.wait()
        xi_start()
        r["labo"][...] = jnp.full((8, 128), label[0, 0].astype(f32))
        lab_up.start()
        load_pj.wait()
        pj_start()
        xi_mid()
        xi_fin()
        xt32 = r["xs"][...].astype(f32)
        inv = lax.rsqrt(jnp.sum(xt32 * xt32, axis=0, keepdims=True) / WI + epsilon)
        r["ivi"][...] = inv
        r["ns"][...] = (xt32 * inv).astype(bf16)
        r["nf"][...] = r["ns"][...].T

    @pl.when(text)
    def _():
        load_xt.wait()
        xt_start()
        xt_mid()
        xt_fin()
        xt32 = r["xt"][...].astype(f32)
        inv = lax.rsqrt(jnp.sum(xt32 * xt32, axis=0, keepdims=True) / WT + epsilon)
        r["ivt"][...] = inv
        r["nt"][...] = (xt32 * inv).astype(bf16)
        r["ntf"][...] = r["nt"][...].T

    @pl.when(image)
    def _():
        load_w1.wait()

        def front(j, carry):
            at = pl.ds(pl.multiple_of(j * 384, 384), 384)
            u = dot(r["nf"][...], r["w1"][:, at])
            val, slope = gelu_both(u)
            r["hi"][ti, :, at] = val.astype(bf16)
            r["gi"][:, at] = slope
            return carry

        lax.fori_loop(0, FI // 384, front, 0)

    @pl.when(text)
    def _():
        load_t1.wait()

        for at in (slice(0, 256), slice(256, 512), slice(512, 640)):
            val, slope = gelu_both(dot(r["ntf"][...], r["w1"][0:WT, at]))
            r["ht"][:, at] = val.astype(bf16)
            r["gt"][:, at] = slope

    @pl.when(image)
    def _():
        load_w2.wait()

        def back(j, carry):
            at = pl.ds(pl.multiple_of(j * 256, 256), 256)
            r["p2i"][:, at] = dot(r["hi"][ti], r["w2"][:, at])
            return carry

        lax.fori_loop(0, WI // 256, back, 0)

    @pl.when(text)
    def _():
        load_t2.wait()

        def back(j, carry):
            at = pl.ds(pl.multiple_of(j * 384, 384), 384)
            r["p2t"][:, at] = dot(r["ht"][...], r["w2"][0:FT, at])
            return carry

        lax.fori_loop(0, WT // 384, back, 0)
        for s in range(3):
            arrive(r["lab"].at[d, s], lab_b + s)
        for c in lab_out:
            c.start()

    @pl.when(image)
    def _():
        r["xf"][...] = r["xs"][...].T
        s2i_start()
        s2i_mid()
        part = s2i_fin()
        rows = pl.ds(pl.multiple_of(m * IQ, IQ), IQ)
        x = r["xf"][rows, :].astype(f32)
        blended = (x + (part + r["rx2i"][...].astype(f32))).astype(bf16)
        for k in range(NM):
            r["bl"][m, k] = blended[:, k * IS:(k + 1) * IS]
        pj_mid()
        pj_fin()
        projected = dot_t(blended, r["pj"][...])
        length = jnp.sqrt(jnp.sum(projected * projected, axis=1, keepdims=True))
        r["pr"][...] = projected
        r["ln"][...] = length
        r["ei"][m] = (projected / length).astype(bf16)
        star_img.start()
        ei_start()
        bl_start()

    @pl.when(text)
    def _():
        r["xtf"][...] = r["xt"][...].T
        s2t_start()
        s2t_mid()
        part = s2t_fin()
        rows = pl.ds(pl.multiple_of(m * TQ, TQ), TQ)
        x = r["xtf"][rows, :].astype(f32)
        blended = x + (part + r["rx2t"][...].astype(f32))
        length = jnp.sqrt(jnp.sum(blended * blended, axis=1, keepdims=True))
        r["tb"][...] = blended
        r["tl"][...] = length
        r["et"][m] = (blended / length).astype(bf16)
        for c in star_txt:
            c.start()
        et_start()

    for c in range(3):
        arrive(cols.at[d, pl.ds(IQ * c, IQ)], star + c)
        for copy in ring_out[c]:
            copy.start()

    @pl.when(image)
    def _():
        ei_mid()
        hid_si()
        nor_si()
        bl_mid()
        ei_fin()

    @pl.when(text)
    def _():
        et_mid()
        hid_st()
        nor_st()
        et_fin()
        for dd in others_d:
            arrive(r["lab"].at[dd], lab_d + dd)

    scale_v, bias_v, loss_v = scale[0, 0], bias[0, 0], loss[0, 0]

    def weight(scores, positive):
        logits = scale_v * scores + bias_v
        signed = jnp.where(positive, 1.0, -1.0).astype(f32)
        grad = -loss_v * signed * jax.nn.sigmoid(-signed * logits)
        return (scale_v * grad).astype(bf16)

    def block_ready(dd):
        for c in range(3):
            arrive(cols.at[dd, pl.ds(IQ * c, IQ)], ring + ND * c + dd)

    @pl.when(image)
    def _():
        emb = r["ei"][...].reshape(IR, WT)
        row = (t * ND + d) * IR + lax.broadcasted_iota(jnp.int32, (IR, TQ), 0) + label[0, 0]
        target = jnp.where(row >= BATCH, row - BATCH, row)
        lane = lax.broadcasted_iota(jnp.int32, (IR, TQ), 1)

        def block(dd):
            pw = weight(dot_t(emb, cols[dd]), target == lane + (dd * TR + m * TQ))
            return dot(pw, cols[dd])

        r["q4t"][0:IR] = block(d)

        def step(k, carry):
            dd = (d + k) % ND
            block_ready(dd)
            r["q4t"][0:IR] += block(dd)
            return carry

        lax.fori_loop(1, ND, step, 0)

    @pl.when(text)
    def _():
        emb = r["et"][...].reshape(TR, WT)
        row = d * TR + lax.broadcasted_iota(jnp.int32, (TR, TQ), 0)
        lane = lax.broadcasted_iota(jnp.int32, (1, TQ), 1)
        part = lane // IQ

        def block(dd):
            off = r["lab"][dd]
            off = jnp.where(part == 0, off[0, :1, :TQ], jnp.where(part == 1, off[1, :1, :TQ], off[2, :1, :TQ]))
            own = (part * ND + dd) * IR + m * IQ + lane % IQ
            target = own + off.astype(jnp.int32)
            target = jnp.where(target >= BATCH, target - BATCH, target)
            pw = weight(dot_t(emb, cols[dd]), row == target)
            return dot(pw, cols[dd])

        r["q4t"][...] = block(d)

        def step(k, carry):
            dd = (d + k) % ND
            block_ready(dd)
            r["q4t"][...] += block(dd)
            return carry

        lax.fori_loop(1, ND, step, 0)

    @pl.when(image)
    def _():
        s4i_start()
        s4i_mid()
        part = s4i_fin()
        grad = part + r["rx4t"][0:IQ].astype(f32)
        length = r["ln"][...]
        direction = r["pr"][...] / length
        pg = ((grad - direction * jnp.sum(direction * grad, axis=1, keepdims=True)) / length).astype(bf16)
        r["bfi"][m] = dot(pg, r["pj"][...]).astype(bf16)
        r["pgf"][...] = pg

    @pl.when(text)
    def _():
        s4t_start()
        s4t_mid()
        part = s4t_fin()
        grad = part + r["rx4t"][...].astype(f32)
        length = r["tl"][...]
        direction = r["tb"][...] / length
        blended_grad = (grad - direction * jnp.sum(direction * grad, axis=1, keepdims=True)) / length
        r["bft"][m] = blended_grad.astype(bf16)

    @pl.when(image)
    def _():
        bi_start()
        for k in range(NM):
            r["pgs"][k] = r["pgf"][:, k * TS:(k + 1) * TS]
        r["pgr"][m] = r["pgs"][m]
        for c in pg_out:
            c.start()
        bl_fin()
        blx_si()
        r["al"][ti] = r["bl"][:, ti]
        r["an"][ti] = r["ns"][pl.ds(pl.multiple_of(ti * IS, IS), IS), :]
        bi_mid()
        bi_fin()
        r["bsi"][...] = r["bfi"][...].reshape(IR, WI).T
        bg_si()
        r["ab"][ti] = r["bsi"][pl.ds(pl.multiple_of(ti * IS, IS), IS), :]

    @pl.when(text)
    def _():
        bt_start()
        r["ant"][...] = r["nt"][(NT - 1) * TS:]
        bt_mid()
        bt_fin()
        r["bst"][...] = r["bft"][...].reshape(TR, WT).T
        bg_st()
        r["abt"][...] = r["bst"][(NT - 1) * TS:]

    @pl.when(image)
    def _():
        for j in range(FI // FC):
            for lo, wide in ((0, 384), (384, 256)):
                at = slice(j * FC + lo, j * FC + lo + wide)
                hg = dot_t(r["bfi"][...].reshape(IR, WI), r["w2"][at, :])
                r["ki"][ti, :, at] = (hg * r["gi"][:, at]).astype(bf16)
            pre[j][0]()
        for dev in (opp, diag, sib):
            arrive(r["pgr"].at[dev[2]], pgb + dev[2])
        pgx_si()
        r["bj"][ti] = r["pgr"][...]

    @pl.when(text)
    def _():
        for at in (slice(0, 384), slice(384, 640)):
            hg = dot_t(r["bft"][...].reshape(TR, WT), r["w2"][at, 0:WT])
            r["kt"][:, at] = (hg * r["gt"][:, at]).astype(bf16)
        pre[0][1]()

    def by_z(g, own, dst, at):
        for p in range(4):
            pair = [g[(q * 4 + p) * own:(q * 4 + p + 1) * own] for q in range(2)]
            dst(p)[:, at] = jnp.concatenate(pair, axis=0).astype(bf16)

    def by_y(g, own, dst, at):
        for p in range(2):
            dst(p)[:, at] = g[p * 4 * own:(p + 1) * 4 * own].astype(bf16)

    def product(lhs, rhs, put, own, dst, begin, width):
        done = 0
        while done < width:
            wide = min(384, width - done)
            put(dot(lhs, rhs(slice(begin + done, begin + done + wide))), own, dst, slice(done, done + wide))
            done += wide

    def three(name):
        return jnp.concatenate([r[name][s] for s in range(3)], axis=1)

    hid_fin()
    bg_fin()
    for j in range(FI // FC):
        product(three("ab"), lambda at: r["hi"][:, :, at].reshape(3 * IR, at.stop - at.start),
                by_z, IO, lambda p, j=j: sb2(j, p), j * FC, FC)
        w2_steps[j][0]()
    product(r["abt"][...], lambda at: r["ht"][:, at], by_y, TO, lambda p: r["sbt2"].at[p], 0, FT)
    t2_steps[0][0]()

    @pl.when(image)
    def _():
        total = jnp.zeros((1, IR), f32)
        for k in range(NM):
            g = dot_t(r["w1"][k * IS:(k + 1) * IS, :], r["ki"][ti])
            total = total + jnp.sum(r["ns"][k * IS:(k + 1) * IS, :].astype(f32) * g, axis=0, keepdims=True)
            r["g6i"][k, 0:IS, :] = g
        tail = jnp.broadcast_to(total, (16, IR))
        for k in range(NM):
            r["g6i"][k, IS:IG, :] = tail
        s6i_start()

    @pl.when(text)
    def _():
        total = jnp.zeros((1, TR), f32)
        for k in range(NM):
            g = dot_t(r["w1"][k * TS:(k + 1) * TS, 0:FT], r["kt"][...])
            total = total + jnp.sum(r["nt"][k * TS:(k + 1) * TS, :].astype(f32) * g, axis=0, keepdims=True)
            r["g6t"][k, 0:TS, :] = g
        tail = jnp.broadcast_to(total, (16, TR))
        for k in range(NM):
            r["g6t"][k, TS:TG, :] = tail
        s6t_start()

    nor_fin()
    for j in range(FI // FC):
        pre[j][2]()
        product(three("an"), lambda at: r["ki"][:, :, at].reshape(3 * IR, at.stop - at.start),
                by_y, IO, lambda p, j=j: sb1(j, p), j * FC, FC)
        w1_steps[j][0]()
        if j == 0:
            @pl.when(image)
            def _():
                s6i_mid()

            @pl.when(text)
            def _():
                s6t_mid()
        w2_steps[j][1]()
    product(r["ant"][...], lambda at: r["kt"][:, at], by_z, TO, lambda p: r["sbt1"].at[p], 0, FT)
    t1_steps[0][0]()
    blx_fin()
    pgx_fin()
    by_y(dot_rows(r["al"][...].reshape(3 * IR, IS), r["bj"][...].reshape(3 * IR, TS)), IO, lambda p: r["sbj"].at[p], slice(0, TS))
    pj_steps[0][0]()

    @pl.when(image)
    def _():
        part = s6i_fin()
        other = r["rx6i"][...].astype(f32)
        average = (part[IS:IS + 1] + other[IS:IS + 1] + other[IS + 1:IS + 2]) / WI
        grad = part[:IS] + other[:IS]
        inv = r["ivi"][...]
        normed = r["xs"][mi, :].astype(f32) * inv
        o_img[0] = r["bsi"][mi, :].astype(f32) + (grad - normed * average) * inv
        o_txt[0] = jnp.zeros((TS, TR), f32)

    @pl.when(text)
    def _():
        part = s6t_fin()
        other = r["rx6t"][...].astype(f32)
        average = (part[TS:TS + 1] + other[TS:TS + 1] + other[TS + 1:TS + 2]) / WT
        grad = part[:TS] + other[:TS]
        inv = r["ivt"][...]
        normed = r["xt"][mt, :].astype(f32) * inv
        o_txt[0] = r["bst"][mt, :].astype(f32) + (grad - normed * average) * inv
        o_img[0] = jnp.zeros((IS, IR), f32)

    t2_steps[0][1]()
    for j in range(FI // FC):
        w1_steps[j][1]()
    t1_steps[0][1]()
    pj_steps[0][1]()
    for j in range(FI // FC):
        w2_steps[j][2](o_w2)
    t2_steps[0][2](o_t2)
    for j in range(FI // FC):
        w1_steps[j][2](o_w1)
    t1_steps[0][2](o_t1)
    pj_steps[0][2](o_pj)

    for c in all_sends:
        c.wait_send()

    @pl.when(image)
    def _():
        for c in img_sends:
            c.wait_send()

    @pl.when(text)
    def _():
        for c in txt_sends:
            c.wait_send()


def move(*refs):
    n = len(refs) // 2
    sem = refs[-1]
    copies = [pltpu.make_async_copy(refs[k], refs[n + k], sem.at[k]) for k in range(n)]
    for c in copies:
        c.start()
    for c in copies:
        c.wait()


def per_device(
    image_in, text_in, img_w1, img_w2, img_proj, txt_w1, txt_w2, label_offset,
    logit_scale, logit_bias, loss_scale,
):
    anywhere = pl.BlockSpec(memory_space=pl.ANY)
    scalar = pl.BlockSpec(memory_space=pltpu.SMEM)
    vmem = pl.BlockSpec(memory_space=pltpu.VMEM)
    one = lambda v: v.reshape(1, 1)
    outs = pl.pallas_call(
        step_kernel,
        out_shape=[
            jax.ShapeDtypeStruct((1, IS, IR), f32),
            jax.ShapeDtypeStruct((1, TS, TR), f32),
            jax.ShapeDtypeStruct((IO, FI), f32),
            jax.ShapeDtypeStruct((IO, FI), f32),
            jax.ShapeDtypeStruct((IO, TS), f32),
            jax.ShapeDtypeStruct((TO, FT), f32),
            jax.ShapeDtypeStruct((TO, FT), f32),
        ],
        in_specs=[anywhere] * 7 + [scalar] * 4,
        out_specs=[vmem] * 7,
        scratch_shapes=list(scratch_list().values()),
        compiler_params=pltpu.CompilerParams(
            collective_id=0, has_side_effects=True, vmem_limit_bytes=63 << 20
        ),
        name="step",
    )(
        image_in.swapaxes(1, 2), text_in.swapaxes(1, 2), img_w1, img_w2, img_proj.T, txt_w1, txt_w2, label_offset,
        one(logit_scale), one(logit_bias), one(loss_scale),
    )
    outs = pl.pallas_call(
        move,
        out_shape=[jax.ShapeDtypeStruct(o.shape, o.dtype) for o in outs],
        in_specs=[anywhere] * len(outs),
        out_specs=[vmem] * len(outs),
        scratch_shapes=[pltpu.SemaphoreType.DMA((len(outs),))],
        name="place",
    )(*outs)
    g_img, g_txt, g_w1, g_w2, g_pj, g_t1, g_t2 = outs
    return (g_img.swapaxes(1, 2), g_txt.swapaxes(1, 2), g_w1, g_w2.T, g_pj, g_t1, g_t2.T)


def solution(mesh):
    return jax.shard_map(
        per_device,
        mesh=mesh,
        in_specs=(
            P("tower", "dp", "mp"),
            P("tower", "dp", "mp"),
            P(None, "mp"),
            P("mp", None),
            P(None, "mp"),
            P(None, "mp"),
            P("mp", None),
            P("tower", "dp"),
            P(),
            P(),
            P(),
        ),
        out_specs=(
            P("tower", "dp", "mp"),
            P("tower", "dp", "mp"),
            P(("tower", "dp"), "mp"),
            P("mp", ("tower", "dp")),
            P(("tower", "dp"), "mp"),
            P(("tower", "dp"), "mp"),
            P("mp", ("tower", "dp")),
        ),
        check_vma=False,
    )
```

```python
import functools
import math

import jax
import jax.numpy as jnp
from jax import lax
from jax.experimental import pallas as pl
from jax.experimental.pallas import tpu as pltpu
from jax.sharding import PartitionSpec as P

epsilon = 1e-06
bf16 = jnp.bfloat16
f32 = jnp.float32
MESH = pl.DeviceIdType.MESH
GELU_A = math.sqrt(2.0 / math.pi)
GELU_B = 0.044715

NT = 4
ND = 8
NM = 4
IR = 128
TR = 384
IQ = IR // NM
TQ = TR // NM
WI = 1792
WT = 1152
IS = WI // NM
TS = WT // NM
FI = 1920
FT = 640
BATCH = 3072
IO = WI // 32
TO = WT // 32
IP = 64
TP = 48
IG = IS + 16
TG = TS + 16
FC = 640
N_SEM = 420
LIMIT = None


def dot(a, b):
    return jnp.dot(a, b, preferred_element_type=f32)


def dot_t(a, b):
    return lax.dot_general(a, b, (((1,), (1,)), ((), ())), preferred_element_type=f32)


def dot_rows(a, b):
    return lax.dot_general(a, b, (((0,), (0,)), ((), ())), preferred_element_type=f32)


def gelu_both(u):
    sq = u * u
    th = jnp.tanh(GELU_A * u * (1.0 + GELU_B * sq))
    half = 0.5 * (1.0 + th)
    slope = half + 0.5 * u * (1.0 - th * th) * (GELU_A * (1.0 + 3.0 * GELU_B * sq))
    return u * half, slope


def scratch_list():
    v = pltpu.VMEM
    return dict(
        w1=v((WI, FI), bf16),
        w2=v((FI, WI), bf16),
        pj=v((WT, WI), bf16),
        xs=v((WI, IR), bf16),
        xt=v((WT, TR), bf16),
        xf=v((IR, WI), bf16),
        xtf=v((TR, WT), bf16),
        ns=v((WI, IR), bf16),
        nt=v((WT, TR), bf16),
        nf=v((IR, WI), bf16),
        ntf=v((TR, WT), bf16),
        ivi=v((1, IR), f32),
        ivt=v((1, TR), f32),
        hi=v((3, IR, FI), bf16),
        ht=v((TR, FT), bf16),
        gi=v((IR, FI), f32),
        gt=v((TR, FT), f32),
        p2i=v((IR, WI), f32),
        p2t=v((TR, WT), f32),
        rc2i=v((2, IQ, WI), f32),
        rc2t=v((2, TQ, WT), f32),
        st2i=v((IQ, WI), bf16),
        st2t=v((TQ, WT), bf16),
        rx2i=v((IQ, WI), bf16),
        rx2t=v((TQ, WT), bf16),
        tb=v((TQ, WT), f32),
        tl=v((TQ, 1), f32),
        bl=v((NM, NM, IQ, IS), bf16),
        pr=v((IQ, WT), f32),
        ln=v((IQ, 1), f32),
        ei=v((NM, IQ, WT), bf16),
        et=v((NM, TQ, WT), bf16),
        cols=v((ND, TQ, WT), bf16),
        lab=v((ND, 3, 8, 128), f32),
        labo=v((8, 128), f32),
        q4t=v((TR, WT), f32),
        rc4t=v((2, TQ, WT), f32),
        st4t=v((TQ, WT), bf16),
        rx4t=v((TQ, WT), bf16),
        bfi=v((NM, IQ, WI), bf16),
        bft=v((NM, TQ, WT), bf16),
        pgf=v((IQ, WT), bf16),
        pgs=v((NM, IQ, TS), bf16),
        pgr=v((NM, IQ, TS), bf16),
        bsi=v((WI, IR), bf16),
        bst=v((WT, TR), bf16),
        an=v((3, IS, IR), bf16),
        ant=v((TS, TR), bf16),
        ab=v((3, IS, IR), bf16),
        abt=v((TS, TR), bf16),
        al=v((3, NM, IQ, IS), bf16),
        bj=v((3, NM, IQ, TS), bf16),
        ki=v((3, IR, FI), bf16),
        kt=v((TR, FT), bf16),
        g6i=v((NM, IG, IR), f32),
        g6t=v((NM, TG, TR), f32),
        rc6i=v((2, IG, IR), f32),
        rc6t=v((2, TG, TR), f32),
        st6i=v((IG, IR), bf16),
        st6t=v((TG, TR), bf16),
        rx6i=v((IG, IR), bf16),
        rx6t=v((TG, TR), bf16),
        ra1=v((2, 4 * IO, FI), bf16),
        sc1=v((4, IP, FI), bf16),
        rc1=v((4, IP, FI), bf16),
        ra2=v((4, 2 * IO, FI), bf16),
        sc2=v((2, IP, FI), bf16),
        rc2=v((2, IP, FI), bf16),
        sbj=v((2, 4 * IO, TS), bf16),
        raj=v((2, 4 * IO, TS), bf16),
        scj=v((4, IP, TS), bf16),
        rcj=v((4, IP, TS), bf16),
        sbt1=v((4, 2 * TO, FT), bf16),
        rat1=v((4, 2 * TO, FT), bf16),
        sct1=v((2, TP, FT), bf16),
        rct1=v((2, TP, FT), bf16),
        sbt2=v((2, 4 * TO, FT), bf16),
        rat2=v((2, 4 * TO, FT), bf16),
        sct2=v((4, TP, FT), bf16),
        rct2=v((4, TP, FT), bf16),
        sem=pltpu.SemaphoreType.DMA((N_SEM,)),
    )


NAMES = list(scratch_list())


def step_kernel(
    img_in, txt_in, w1_in, w2_in, pj_in, tw1_in, tw2_in, label, scale, bias, loss,
    o_img, o_txt, o_w1, o_w2, o_pj, o_t1, o_t2, *scratch
):
    r = dict(zip(NAMES, scratch))
    sem = r["sem"]
    used = [0]
    t = lax.axis_index("tower")
    d = lax.axis_index("dp")
    m = lax.axis_index("mp")
    core = m % 2
    high = m // 2
    ms = m + 1 - 2 * core
    mo = (m + 2) % NM
    md = (ms + 2) % NM
    text = t == NT - 1
    image = t != NT - 1
    ti = jnp.minimum(t, 2)
    sib, opp, diag = (t, d, ms), (t, d, mo), (t, d, md)
    dy = d // 4
    dz = d % 4
    flip = (t, (d + 4) % ND, mo)
    others_t = [((t + k) % NT, d, m) for k in (1, 2, 3)]
    order_d = (4, 1, 3, 5, 7, 2, 6)
    others_d = [(d + k) % ND for k in order_d]

    def take(n):
        first = used[0]
        used[0] += n
        assert used[0] <= N_SEM
        return first

    img_sends, txt_sends, all_sends = [], [], []
    plans = []

    class Tracked:
        def __init__(self, copy, group):
            self.copy, self.group = copy, group

        def start(self):
            self.copy.start()
            self.group.append(self.copy)

    def plan(group, *steps):
        entry = {"group": group, "left": list(steps), "begun": False}
        plans.append(entry)

        def runner(step):
            def run(*args):
                entry["begun"] = True
                entry["left"].remove(step)
                return step(*args)
            return run

        return [runner(s) for s in steps]

    def send(src, dst, arrived, dev, group):
        copy = pltpu.make_async_remote_copy(
            src_ref=src, dst_ref=dst, send_sem=sem.at[take(1)], recv_sem=sem.at[arrived],
            device_id=dev, device_id_type=MESH,
        )
        return Tracked(copy, group)

    def arrive(dst, arrived):
        pltpu.make_async_remote_copy(
            src_ref=dst, dst_ref=dst, send_sem=sem.at[0], recv_sem=sem.at[arrived],
            device_id=sib, device_id_type=MESH,
        ).wait_recv()

    def gather_mp(slot, group):
        b = take(NM)
        to_opp = send(slot(m), slot(m), b + m, opp, group)
        to_sib = send(slot(m), slot(m), b + m, sib, group)
        pass_on = send(slot(mo), slot(mo), b + mo, sib, group)

        def start():
            to_opp.start()
            to_sib.start()

        def middle():
            arrive(slot(mo), b + mo)
            pass_on.start()

        def finish():
            arrive(slot(ms), b + ms)
            arrive(slot(md), b + md)

        return plan(group, start, middle, finish)

    def sum_mp(quarter, rc, st, rx, group, pack=None):
        b = take(3)
        first, second = 1 - high, high
        s1 = send(quarter(2 * first + 1 - core), rc.at[first], b + first, sib, group)
        s2 = send(quarter(2 * second + 1 - core), rc.at[second], b + second, sib, group)
        cross = send(st, rx, b + 2, opp, group)

        def start():
            s1.start()
            s2.start()

        def middle():
            arrive(rc.at[first], b + first)
            part = quarter(2 * first + core)[...] + rc[first]
            st[...] = part.astype(bf16) if pack is None else pack(part)
            cross.start()

        def finish():
            arrive(rc.at[second], b + second)
            mine = quarter(2 * second + core)[...] + rc[second]
            arrive(rx, b + 2)
            return mine

        return plan(group, start, middle, finish)

    def exchange_x(src_img, dst_img, src_txt, dst_txt):
        b = take(NT)
        ci = [send(src_img(dev[0]), dst_img(ti), b + ti, dev, img_sends) for dev in others_t]
        ct = [send(src_txt(dev[0]), dst_txt, b + 3, dev, txt_sends) for dev in others_t] if src_txt else []

        def start_img():
            for c in ci:
                c.start()

        def start_txt():
            for c in ct:
                c.start()

        def finish():
            for s in range(3):
                @pl.when(t != s)
                def _(s=s):
                    arrive(dst_img(s), b + s)
            if src_txt:
                @pl.when(image)
                def _():
                    arrive(dst_txt, b + 3)

        return plan(all_sends, start_img, start_txt, finish)

    def scatter_dp(mode, own, padded, spans, first, first_in, second, second_in):
        along_y = mode == "y"
        parts = 2 if along_y else 4
        me, rest = (dy, dz) if along_y else (dz, dy)

        def dev_first(p):
            return (t, p * 4 + dz, m) if along_y else (t, dy * 4 + p, m)

        def dev_second(p):
            return (t, dy * 4 + p, m) if along_y else (t, p * 4 + dz, m)

        steps = []
        for j, span in enumerate(spans):
            b1, b2 = take(4), take(4)
            one = [(me + k) % parts for k in range(1, parts)]
            two = [(rest + k) % (8 // parts) for k in range(1, 8 // parts)]
            c1 = [send(first(j, p), first_in.at[me, :, span], b1 + me, dev_first(p), all_sends) for p in one]
            c2 = [send(second.at[p, :, span], second_in.at[rest, :, span], b2 + rest, dev_second(p), all_sends)
                  for p in two]

            def start(c1=c1):
                for c in c1:
                    c.start()

            def middle(j=j, span=span, one=one, b1=b1, c2=c2):
                total = first(j, me)[...].astype(f32)
                for p in one:
                    arrive(first_in.at[p, :, span], b1 + p)
                    total = total + first_in[p, :, span].astype(f32)
                pad = jnp.zeros((padded - own, total.shape[1]), f32)
                for k in range(8 // parts):
                    piece = jnp.concatenate([total[k * own:(k + 1) * own], pad], axis=0)
                    second[k, :, span] = piece.astype(bf16)
                for c in c2:
                    c.start()

            def finish(out=None, span=span, two=two, b2=b2):
                total = second[rest, :, span].astype(f32)
                for p in two:
                    arrive(second_in.at[p, :, span], b2 + p)
                    total = total + second_in[p, :, span].astype(f32)
                if out is not None:
                    out[:, span] = total[:own]

            steps.append(plan(all_sends, start, middle, finish))
        return steps

    lb = take(5)
    mi = pl.ds(pl.multiple_of(m * IS, IS), IS)
    mt = pl.ds(pl.multiple_of(m * TS, TS), TS)
    load_xi = pltpu.make_async_copy(img_in.at[0], r["xs"].at[mi], sem.at[lb])
    load_xt = pltpu.make_async_copy(txt_in.at[0], r["xt"].at[mt], sem.at[lb + 1])
    load_w1 = pltpu.make_async_copy(w1_in, r["w1"], sem.at[lb + 2])
    load_w2 = pltpu.make_async_copy(w2_in, r["w2"], sem.at[lb + 3])
    load_pj = pltpu.make_async_copy(pj_in, r["pj"].at[mt], sem.at[lb + 4])
    tw1 = r["w1"].at[pl.ds(0, WT), pl.ds(0, FT)]
    tw2 = r["w2"].at[pl.ds(0, FT), pl.ds(0, WT)]
    load_t1 = pltpu.make_async_copy(tw1_in, tw1, sem.at[lb + 2])
    load_t2 = pltpu.make_async_copy(tw2_in, tw2, sem.at[lb + 3])

    xi_start, xi_mid, xi_fin = gather_mp(lambda i: r["xs"].at[pl.ds(pl.multiple_of(i * IS, IS), IS)], img_sends)
    xt_start, xt_mid, xt_fin = gather_mp(lambda i: r["xt"].at[pl.ds(pl.multiple_of(i * TS, TS), TS)], txt_sends)
    def head_piece(i, z):
        row = pl.multiple_of(i * TS + (z // 2) * (TS // 2), TS // 2)
        lane = pl.multiple_of((z % 2) * (WI // 2), WI // 2)
        return r["pj"].at[pl.ds(row, TS // 2), pl.ds(lane, WI // 2)]

    def head_slice(i):
        return r["pj"].at[pl.ds(pl.multiple_of(i * TS, TS), TS)]

    other_z = [(dz + k) % 4 for k in (1, 3, 2)]
    pjb, pjs, pjz = take(1), take(5), take(4)
    pj_cross = send(head_piece(m, dz), head_piece(m, dz), pjb, flip, img_sends)
    pj_own = send(head_slice(m), head_slice(m), pjs + 4, sib, img_sends)
    pj_spread = [send(head_piece(mo, dz), head_piece(mo, dz), pjz + dz, (t, dy * 4 + z, m), img_sends) for z in other_z]
    pj_pass = [send(head_piece(mo, z), head_piece(mo, z), pjs + z, sib, img_sends) for z in [dz] + other_z]

    def pj_start():
        pj_cross.start()
        pj_own.start()

    def pj_mid():
        arrive(head_piece(mo, dz), pjb)
        for c in pj_spread:
            c.start()
        pj_pass[0].start()

    def pj_fin():
        for z, c in zip(other_z, pj_pass[1:]):
            arrive(head_piece(mo, z), pjz + z)
            c.start()
        arrive(head_slice(ms), pjs + 4)
        for z in range(4):
            arrive(head_piece(md, z), pjs + z)

    pj_start, pj_mid, pj_fin = plan(img_sends, pj_start, pj_mid, pj_fin)

    lab_b = take(3)
    lab_up = send(r["labo"], r["lab"].at[d, ti], lab_b + ti, (NT - 1, d, m), img_sends)
    lab_d = take(ND)
    lab_out = [send(r["lab"].at[d], r["lab"].at[d], lab_d + d, (t, dd, m), txt_sends) for dd in others_d]

    s2i_start, s2i_mid, s2i_fin = sum_mp(lambda q: r["p2i"].at[pl.ds(q * IQ, IQ)], r["rc2i"], r["st2i"], r["rx2i"], img_sends)
    s2t_start, s2t_mid, s2t_fin = sum_mp(lambda q: r["p2t"].at[pl.ds(q * TQ, TQ)], r["rc2t"], r["st2t"], r["rx2t"], txt_sends)

    cols = r["cols"]
    star = take(3)
    star_img = send(r["ei"].at[m], cols.at[d, pl.ds(IQ * ti, IQ)], star + ti, (NT - 1, d, m), img_sends)
    star_txt = [
        send(r["et"].at[m, pl.ds(IQ * c, IQ)], cols.at[d, pl.ds(IQ * c, IQ)], star + c, dev, txt_sends)
        for c in range(3) for dev in others_t
    ]
    ring = take(3 * ND)
    ring_out = [
        [send(cols.at[d, pl.ds(IQ * c, IQ)], cols.at[d, pl.ds(IQ * c, IQ)], ring + ND * c + d, (t, dd, m), all_sends)
         for dd in others_d]
        for c in range(3)
    ]
    ei_start, ei_mid, ei_fin = gather_mp(lambda i: r["ei"].at[i], img_sends)
    et_start, et_mid, et_fin = gather_mp(lambda i: r["et"].at[i], txt_sends)
    bl_start, bl_mid, bl_fin = gather_mp(lambda i: r["bl"].at[i], img_sends)
    hid = []
    for j in range(FI // FC):
        at = slice(j * FC, (j + 1) * FC)
        hid.append(exchange_x(
            lambda s, at=at: r["hi"].at[ti, :, at], lambda s, at=at: r["hi"].at[s, :, at],
            (lambda s: r["ht"]) if j == 0 else None, r["ht"]))
    nor_si, nor_st, nor_fin = exchange_x(
        lambda s: r["ns"].at[pl.ds(s * IS, IS)], lambda s: r["an"].at[s], lambda s: r["nt"].at[pl.ds(s * TS, TS)], r["ant"])
    blx_si, _, blx_fin = exchange_x(
        lambda s: r["bl"].at[:, s], lambda s: r["al"].at[s], None, None)
    s4i_start, s4i_mid, s4i_fin = sum_mp(lambda q: r["q4t"].at[pl.ds(q * IQ, IQ)], r["rc4t"].at[:, 0:IQ], r["st4t"].at[0:IQ], r["rx4t"].at[0:IQ], img_sends)
    s4t_start, s4t_mid, s4t_fin = sum_mp(lambda q: r["q4t"].at[pl.ds(q * TQ, TQ)], r["rc4t"], r["st4t"], r["rx4t"], txt_sends)
    bi_start, bi_mid, bi_fin = gather_mp(lambda i: r["bfi"].at[i], img_sends)
    bt_start, bt_mid, bt_fin = gather_mp(lambda i: r["bft"].at[i], txt_sends)
    pgb = take(NM)
    pg_out = [
        send(r["pgs"].at[dev[2]], r["pgr"].at[m], pgb + m, dev, img_sends) for dev in (opp, diag, sib)
    ]
    pgx_si, _, pgx_fin = exchange_x(lambda s: r["pgr"], lambda s: r["bj"].at[s], None, None)
    bg_si, bg_st, bg_fin = exchange_x(
        lambda s: r["bsi"].at[pl.ds(s * IS, IS)], lambda s: r["ab"].at[s], lambda s: r["bst"].at[pl.ds(s * TS, TS)], r["abt"])
    pre = []
    for j in range(FI // FC):
        at = slice(j * FC, (j + 1) * FC)
        pre.append(exchange_x(
            lambda s, at=at: r["ki"].at[ti, :, at], lambda s, at=at: r["ki"].at[s, :, at],
            (lambda s: r["kt"]) if j == 0 else None, r["kt"]))

    def packer(width):
        def pack(part):
            sums = part[width:]
            top = sums.astype(bf16).astype(f32)
            at = lax.broadcasted_iota(jnp.int32, sums.shape, 0)
            tail = jnp.where(at == 1, sums[0:1] - top[0:1], top)
            return jnp.concatenate([part[:width], tail], axis=0).astype(bf16)
        return pack

    s6i_start, s6i_mid, s6i_fin = sum_mp(lambda q: r["g6i"].at[q], r["rc6i"], r["st6i"], r["rx6i"], img_sends, packer(IS))
    s6t_start, s6t_mid, s6t_fin = sum_mp(lambda q: r["g6t"].at[q], r["rc6t"], r["st6t"], r["rx6t"], txt_sends, packer(TS))
    spans = [slice(j * FC, (j + 1) * FC) for j in range(FI // FC)]
    whole_t = [slice(0, FT)]
    whole_j = [slice(0, TS)]
    def sb2(j, p):
        return r["w2"].at[pl.ds(pl.multiple_of(j * 8 * IO + p * 2 * IO, 2 * IO), 2 * IO), 0:FC]

    def sb1(j, p):
        return r["w1"].at[pl.ds(pl.multiple_of(p * 4 * IO, 4 * IO), 4 * IO), spans[j]]

    w2_steps = scatter_dp(
        "z", IO, IP, spans, sb2, r["ra2"], r["sc2"], r["rc2"])
    w1_steps = scatter_dp(
        "y", IO, IP, spans, sb1, r["ra1"], r["sc1"], r["rc1"])
    t2_steps = scatter_dp("y", TO, TP, whole_t, lambda j, p: r["sbt2"].at[p], r["rat2"], r["sct2"], r["rct2"])
    t1_steps = scatter_dp("z", TO, TP, whole_t, lambda j, p: r["sbt1"].at[p], r["rat1"], r["sct1"], r["rct1"])
    pj_steps = scatter_dp("y", IO, IP, whole_j, lambda j, p: r["sbj"].at[p], r["raj"], r["scj"], r["rcj"])

    @pl.when(image)
    def _():
        load_xi.start()
        load_w1.start()
        load_w2.start()
        load_pj.start()

    @pl.when(text)
    def _():
        load_xt.start()
        load_t1.start()
        load_t2.start()

    barrier = pltpu.get_barrier_semaphore()
    partners = [sib, opp, diag, flip] + others_t + [(t, dd, m) for dd in others_d]
    for dev in partners:
        pl.semaphore_signal(barrier, inc=1, device_id=dev, device_id_type=MESH)
    pl.semaphore_wait(barrier, len(partners))

    @pl.when(image)
    def _():
        load_xi.wait()
        xi_start()
        r["labo"][...] = jnp.full((8, 128), label[0, 0].astype(f32))
        lab_up.start()
        load_pj.wait()
        pj_start()
        xi_mid()
        xi_fin()
        xt32 = r["xs"][...].astype(f32)
        inv = lax.rsqrt(jnp.sum(xt32 * xt32, axis=0, keepdims=True) / WI + epsilon)
        r["ivi"][...] = inv
        r["ns"][...] = (xt32 * inv).astype(bf16)
        nor_si()
        r["nf"][...] = r["ns"][...].T

    @pl.when(text)
    def _():
        load_xt.wait()
        xt_start()
        xt_mid()
        xt_fin()
        xt32 = r["xt"][...].astype(f32)
        inv = lax.rsqrt(jnp.sum(xt32 * xt32, axis=0, keepdims=True) / WT + epsilon)
        r["ivt"][...] = inv
        r["nt"][...] = (xt32 * inv).astype(bf16)
        nor_st()
        r["ntf"][...] = r["nt"][...].T

    @pl.when(image)
    def _():
        load_w1.wait()

        def front(j, carry):
            at = pl.ds(pl.multiple_of(j * 384, 384), 384)
            u = dot(r["nf"][...], r["w1"][:, at])
            val, slope = gelu_both(u)
            r["hi"][ti, :, at] = val.astype(bf16)
            r["gi"][:, at] = slope
            return carry

        lax.fori_loop(0, FI // 384, front, 0)

    @pl.when(text)
    def _():
        load_t1.wait()

        for at in (slice(0, 256), slice(256, 512), slice(512, 640)):
            val, slope = gelu_both(dot(r["ntf"][...], r["w1"][0:WT, at]))
            r["ht"][:, at] = val.astype(bf16)
            r["gt"][:, at] = slope

    @pl.when(image)
    def _():
        hid[0][0]()
        hid[1][0]()
        load_w2.wait()

        def back(j, carry):
            at = pl.ds(pl.multiple_of(j * 256, 256), 256)
            r["p2i"][:, at] = dot(r["hi"][ti], r["w2"][:, at])
            return carry

        lax.fori_loop(0, WI // 256, back, 0)

    @pl.when(text)
    def _():
        load_t2.wait()

        def back(j, carry):
            at = pl.ds(pl.multiple_of(j * 384, 384), 384)
            r["p2t"][:, at] = dot(r["ht"][...], r["w2"][0:FT, at])
            return carry

        lax.fori_loop(0, WT // 384, back, 0)
        for s in range(3):
            arrive(r["lab"].at[d, s], lab_b + s)
        for c in lab_out:
            c.start()

    @pl.when(image)
    def _():
        s2i_start()
        pj_mid()
        r["xf"][...] = r["xs"][...].T
        s2i_mid()
        part = s2i_fin()
        rows = pl.ds(pl.multiple_of(m * IQ, IQ), IQ)
        x = r["xf"][rows, :].astype(f32)
        blended = (x + (part + r["rx2i"][...].astype(f32))).astype(bf16)
        for k in range(NM):
            r["bl"][m, k] = blended[:, k * IS:(k + 1) * IS]
        pj_fin()
        projected = dot_t(blended, r["pj"][...])
        length = jnp.sqrt(jnp.sum(projected * projected, axis=1, keepdims=True))
        r["pr"][...] = projected
        r["ln"][...] = length
        r["ei"][m] = (projected / length).astype(bf16)
        star_img.start()
        ei_start()
        bl_start()

    @pl.when(text)
    def _():
        s2t_start()
        r["xtf"][...] = r["xt"][...].T
        s2t_mid()
        part = s2t_fin()
        rows = pl.ds(pl.multiple_of(m * TQ, TQ), TQ)
        x = r["xtf"][rows, :].astype(f32)
        blended = x + (part + r["rx2t"][...].astype(f32))
        length = jnp.sqrt(jnp.sum(blended * blended, axis=1, keepdims=True))
        r["tb"][...] = blended
        r["tl"][...] = length
        r["et"][m] = (blended / length).astype(bf16)
        for c in star_txt:
            c.start()
        et_start()

    for c in range(3):
        arrive(cols.at[d, pl.ds(IQ * c, IQ)], star + c)
        for copy in ring_out[c]:
            copy.start()

    @pl.when(image)
    def _():
        ei_mid()
        hid[2][0]()
        bl_mid()
        ei_fin()

    @pl.when(text)
    def _():
        et_mid()
        hid[0][1]()
        et_fin()
        for dd in others_d:
            arrive(r["lab"].at[dd], lab_d + dd)

    scale_v, bias_v, loss_v = scale[0, 0], bias[0, 0], loss[0, 0]

    def weight(scores, positive):
        logits = scale_v * scores + bias_v
        signed = jnp.where(positive, 1.0, -1.0).astype(f32)
        grad = -loss_v * signed * jax.nn.sigmoid(-signed * logits)
        return (scale_v * grad).astype(bf16)

    def block_ready(dd):
        for c in range(3):
            arrive(cols.at[dd, pl.ds(IQ * c, IQ)], ring + ND * c + dd)

    @pl.when(image)
    def _():
        emb = r["ei"][...].reshape(IR, WT)
        row = (t * ND + d) * IR + lax.broadcasted_iota(jnp.int32, (IR, TQ), 0) + label[0, 0]
        target = jnp.where(row >= BATCH, row - BATCH, row)
        lane = lax.broadcasted_iota(jnp.int32, (IR, TQ), 1)

        def block(dd):
            pw = weight(dot_t(emb, cols[dd]), target == lane + (dd * TR + m * TQ))
            return dot(pw, cols[dd])

        r["q4t"][0:IR] = block(d)

        def step(k, carry):
            dd = (d + k) % ND
            block_ready(dd)
            r["q4t"][0:IR] += block(dd)
            return carry

        lax.fori_loop(1, ND, step, 0)

    @pl.when(text)
    def _():
        emb = r["et"][...].reshape(TR, WT)
        row = d * TR + lax.broadcasted_iota(jnp.int32, (TR, TQ), 0)
        lane = lax.broadcasted_iota(jnp.int32, (1, TQ), 1)
        part = lane // IQ

        def block(dd):
            off = r["lab"][dd]
            off = jnp.where(part == 0, off[0, :1, :TQ], jnp.where(part == 1, off[1, :1, :TQ], off[2, :1, :TQ]))
            own = (part * ND + dd) * IR + m * IQ + lane % IQ
            target = own + off.astype(jnp.int32)
            target = jnp.where(target >= BATCH, target - BATCH, target)
            pw = weight(dot_t(emb, cols[dd]), row == target)
            return dot(pw, cols[dd])

        r["q4t"][...] = block(d)

        def step(k, carry):
            dd = (d + k) % ND
            block_ready(dd)
            r["q4t"][...] += block(dd)
            return carry

        lax.fori_loop(1, ND, step, 0)

    @pl.when(image)
    def _():
        s4i_start()
        s4i_mid()
        part = s4i_fin()
        grad = part + r["rx4t"][0:IQ].astype(f32)
        length = r["ln"][...]
        direction = r["pr"][...] / length
        pg = ((grad - direction * jnp.sum(direction * grad, axis=1, keepdims=True)) / length).astype(bf16)
        r["bfi"][m] = dot(pg, r["pj"][...]).astype(bf16)
        r["pgf"][...] = pg

    @pl.when(text)
    def _():
        s4t_start()
        s4t_mid()
        part = s4t_fin()
        grad = part + r["rx4t"][...].astype(f32)
        length = r["tl"][...]
        direction = r["tb"][...] / length
        blended_grad = (grad - direction * jnp.sum(direction * grad, axis=1, keepdims=True)) / length
        r["bft"][m] = blended_grad.astype(bf16)

    @pl.when(image)
    def _():
        bi_start()
        for k in range(NM):
            r["pgs"][k] = r["pgf"][:, k * TS:(k + 1) * TS]
        r["pgr"][m] = r["pgs"][m]
        for c in pg_out:
            c.start()
        bl_fin()
        blx_si()
        r["al"][ti] = r["bl"][:, ti]
        r["an"][ti] = r["ns"][pl.ds(pl.multiple_of(ti * IS, IS), IS), :]
        bi_mid()
        bi_fin()
        r["bsi"][...] = r["bfi"][...].reshape(IR, WI).T
        bg_si()
        r["ab"][ti] = r["bsi"][pl.ds(pl.multiple_of(ti * IS, IS), IS), :]

    @pl.when(text)
    def _():
        bt_start()
        r["ant"][...] = r["nt"][(NT - 1) * TS:]
        bt_mid()
        bt_fin()
        r["bst"][...] = r["bft"][...].reshape(TR, WT).T
        bg_st()
        r["abt"][...] = r["bst"][(NT - 1) * TS:]

    @pl.when(image)
    def _():
        for j in range(FI // FC):
            for lo, wide in ((0, 384), (384, 256)):
                at = slice(j * FC + lo, j * FC + lo + wide)
                hg = dot_t(r["bfi"][...].reshape(IR, WI), r["w2"][at, :])
                r["ki"][ti, :, at] = (hg * r["gi"][:, at]).astype(bf16)
            pre[j][0]()
        for dev in (opp, diag, sib):
            arrive(r["pgr"].at[dev[2]], pgb + dev[2])
        pgx_si()
        r["bj"][ti] = r["pgr"][...]

    @pl.when(text)
    def _():
        for at in (slice(0, 384), slice(384, 640)):
            hg = dot_t(r["bft"][...].reshape(TR, WT), r["w2"][at, 0:WT])
            r["kt"][:, at] = (hg * r["gt"][:, at]).astype(bf16)
        pre[0][1]()

    def by_z(g, own, dst, at):
        for p in range(4):
            pair = [g[(q * 4 + p) * own:(q * 4 + p + 1) * own] for q in range(2)]
            dst(p)[:, at] = jnp.concatenate(pair, axis=0).astype(bf16)

    def by_y(g, own, dst, at):
        for p in range(2):
            dst(p)[:, at] = g[p * 4 * own:(p + 1) * 4 * own].astype(bf16)

    def product(lhs, rhs, put, own, dst, begin, width):
        done = 0
        while done < width:
            wide = min(384, width - done)
            put(dot(lhs, rhs(slice(begin + done, begin + done + wide))), own, dst, slice(done, done + wide))
            done += wide

    def three(name):
        return jnp.concatenate([r[name][s] for s in range(3)], axis=1)

    bg_fin()
    for j in range(FI // FC):
        hid[j][2]()
        product(three("ab"), lambda at: r["hi"][:, :, at].reshape(3 * IR, at.stop - at.start),
                by_z, IO, lambda p, j=j: sb2(j, p), j * FC, FC)
        w2_steps[j][0]()
    product(r["abt"][...], lambda at: r["ht"][:, at], by_y, TO, lambda p: r["sbt2"].at[p], 0, FT)
    t2_steps[0][0]()

    @pl.when(image)
    def _():
        total = jnp.zeros((1, IR), f32)
        for k in range(NM):
            g = dot_t(r["w1"][k * IS:(k + 1) * IS, :], r["ki"][ti])
            total = total + jnp.sum(r["ns"][k * IS:(k + 1) * IS, :].astype(f32) * g, axis=0, keepdims=True)
            r["g6i"][k, 0:IS, :] = g
        tail = jnp.broadcast_to(total, (16, IR))
        for k in range(NM):
            r["g6i"][k, IS:IG, :] = tail
        s6i_start()

    @pl.when(text)
    def _():
        total = jnp.zeros((1, TR), f32)
        for k in range(NM):
            g = dot_t(r["w1"][k * TS:(k + 1) * TS, 0:FT], r["kt"][...])
            total = total + jnp.sum(r["nt"][k * TS:(k + 1) * TS, :].astype(f32) * g, axis=0, keepdims=True)
            r["g6t"][k, 0:TS, :] = g
        tail = jnp.broadcast_to(total, (16, TR))
        for k in range(NM):
            r["g6t"][k, TS:TG, :] = tail
        s6t_start()

    nor_fin()
    for j in range(FI // FC):
        pre[j][2]()
        product(three("an"), lambda at: r["ki"][:, :, at].reshape(3 * IR, at.stop - at.start),
                by_y, IO, lambda p, j=j: sb1(j, p), j * FC, FC)
        w1_steps[j][0]()
        if j == 0:
            @pl.when(image)
            def _():
                s6i_mid()

            @pl.when(text)
            def _():
                s6t_mid()
        w2_steps[j][1]()
    product(r["ant"][...], lambda at: r["kt"][:, at], by_z, TO, lambda p: r["sbt1"].at[p], 0, FT)
    t1_steps[0][0]()
    blx_fin()
    pgx_fin()
    by_y(dot_rows(r["al"][...].reshape(3 * IR, IS), r["bj"][...].reshape(3 * IR, TS)), IO, lambda p: r["sbj"].at[p], slice(0, TS))
    pj_steps[0][0]()

    @pl.when(image)
    def _():
        part = s6i_fin()
        other = r["rx6i"][...].astype(f32)
        average = (part[IS:IS + 1] + other[IS:IS + 1] + other[IS + 1:IS + 2]) / WI
        grad = part[:IS] + other[:IS]
        inv = r["ivi"][...]
        normed = r["xs"][mi, :].astype(f32) * inv
        o_img[0] = r["bsi"][mi, :].astype(f32) + (grad - normed * average) * inv
        o_txt[0] = jnp.zeros((TS, TR), f32)

    @pl.when(text)
    def _():
        part = s6t_fin()
        other = r["rx6t"][...].astype(f32)
        average = (part[TS:TS + 1] + other[TS:TS + 1] + other[TS + 1:TS + 2]) / WT
        grad = part[:TS] + other[:TS]
        inv = r["ivt"][...]
        normed = r["xt"][mt, :].astype(f32) * inv
        o_txt[0] = r["bst"][mt, :].astype(f32) + (grad - normed * average) * inv
        o_img[0] = jnp.zeros((IS, IR), f32)

    t2_steps[0][1]()
    for j in range(FI // FC):
        w1_steps[j][1]()
    t1_steps[0][1]()
    pj_steps[0][1]()
    for j in range(FI // FC):
        w2_steps[j][2](o_w2)
    t2_steps[0][2](o_t2)
    for j in range(FI // FC):
        w1_steps[j][2](o_w1)
    t1_steps[0][2](o_t1)
    pj_steps[0][2](o_pj)

    for c in all_sends:
        c.wait_send()

    @pl.when(image)
    def _():
        for c in img_sends:
            c.wait_send()

    @pl.when(text)
    def _():
        for c in txt_sends:
            c.wait_send()


def move(*refs):
    n = len(refs) // 2
    sem = refs[-1]
    copies = [pltpu.make_async_copy(refs[k], refs[n + k], sem.at[k]) for k in range(n)]
    for c in copies:
        c.start()
    for c in copies:
        c.wait()


def per_device(
    image_in, text_in, img_w1, img_w2, img_proj, txt_w1, txt_w2, label_offset,
    logit_scale, logit_bias, loss_scale,
):
    anywhere = pl.BlockSpec(memory_space=pl.ANY)
    scalar = pl.BlockSpec(memory_space=pltpu.SMEM)
    vmem = pl.BlockSpec(memory_space=pltpu.VMEM)
    one = lambda v: v.reshape(1, 1)
    outs = pl.pallas_call(
        step_kernel,
        out_shape=[
            jax.ShapeDtypeStruct((1, IS, IR), f32),
            jax.ShapeDtypeStruct((1, TS, TR), f32),
            jax.ShapeDtypeStruct((IO, FI), f32),
            jax.ShapeDtypeStruct((IO, FI), f32),
            jax.ShapeDtypeStruct((IO, TS), f32),
            jax.ShapeDtypeStruct((TO, FT), f32),
            jax.ShapeDtypeStruct((TO, FT), f32),
        ],
        in_specs=[anywhere] * 7 + [scalar] * 4,
        out_specs=[vmem] * 7,
        scratch_shapes=list(scratch_list().values()),
        compiler_params=pltpu.CompilerParams(
            collective_id=0, has_side_effects=True, vmem_limit_bytes=63 << 20
        ),
        name="step",
    )(
        image_in.swapaxes(1, 2), text_in.swapaxes(1, 2), img_w1, img_w2, img_proj.T, txt_w1, txt_w2, label_offset,
        one(logit_scale), one(logit_bias), one(loss_scale),
    )
    outs = pl.pallas_call(
        move,
        out_shape=[jax.ShapeDtypeStruct(o.shape, o.dtype) for o in outs],
        in_specs=[anywhere] * len(outs),
        out_specs=[vmem] * len(outs),
        scratch_shapes=[pltpu.SemaphoreType.DMA((len(outs),))],
        name="place",
    )(*outs)
    g_img, g_txt, g_w1, g_w2, g_pj, g_t1, g_t2 = outs
    return (g_img.swapaxes(1, 2), g_txt.swapaxes(1, 2), g_w1, g_w2.T, g_pj, g_t1, g_t2.T)


def solution(mesh):
    return jax.shard_map(
        per_device,
        mesh=mesh,
        in_specs=(
            P("tower", "dp", "mp"),
            P("tower", "dp", "mp"),
            P(None, "mp"),
            P("mp", None),
            P(None, "mp"),
            P(None, "mp"),
            P("mp", None),
            P("tower", "dp"),
            P(),
            P(),
            P(),
        ),
        out_specs=(
            P("tower", "dp", "mp"),
            P("tower", "dp", "mp"),
            P(("tower", "dp"), "mp"),
            P("mp", ("tower", "dp")),
            P(("tower", "dp"), "mp"),
            P(("tower", "dp"), "mp"),
            P("mp", ("tower", "dp")),
        ),
        check_vma=False,
    )
```

```python
import functools
import math

import jax
import jax.numpy as jnp
from jax import lax
from jax.experimental import pallas as pl
from jax.experimental.pallas import tpu as pltpu
from jax.sharding import PartitionSpec as P

epsilon = 1e-06
bf16 = jnp.bfloat16
f32 = jnp.float32
MESH = pl.DeviceIdType.MESH
GELU_A = math.sqrt(2.0 / math.pi)
GELU_B = 0.044715

NT = 4
ND = 8
NM = 4
IR = 128
TR = 384
IQ = IR // NM
TQ = TR // NM
WI = 1792
WT = 1152
IS = WI // NM
TS = WT // NM
FI = 1920
FT = 640
BATCH = 3072
IO = WI // 32
TO = WT // 32
IP = 64
TP = 48
IG = IS + 16
TG = TS + 16
FC = 640
N_SEM = 420
LIMIT = None


def dot(a, b):
    return jnp.dot(a, b, preferred_element_type=f32)


def dot_t(a, b):
    return lax.dot_general(a, b, (((1,), (1,)), ((), ())), preferred_element_type=f32)


def dot_rows(a, b):
    return lax.dot_general(a, b, (((0,), (0,)), ((), ())), preferred_element_type=f32)


def gelu_both(u):
    sq = u * u
    th = jnp.tanh(GELU_A * u * (1.0 + GELU_B * sq))
    half = 0.5 * (1.0 + th)
    slope = half + 0.5 * u * (1.0 - th * th) * (GELU_A * (1.0 + 3.0 * GELU_B * sq))
    return u * half, slope


def scratch_list():
    v = pltpu.VMEM
    return dict(
        w1=v((WI, FI), bf16),
        w2=v((FI, WI), bf16),
        pj=v((WT, WI), bf16),
        xs=v((WI, IR), bf16),
        xt=v((WT, TR), bf16),
        xf=v((IR, WI), bf16),
        xtf=v((TR, WT), bf16),
        ns=v((WI, IR), bf16),
        nt=v((WT, TR), bf16),
        nf=v((IR, WI), bf16),
        ntf=v((TR, WT), bf16),
        ivi=v((1, IR), f32),
        ivt=v((1, TR), f32),
        hi=v((3, IR, FI), bf16),
        ht=v((TR, FT), bf16),
        gi=v((IR, FI), f32),
        gt=v((TR, FT), f32),
        p2i=v((IR, WI), f32),
        p2t=v((TR, WT), f32),
        rc2i=v((2, IQ, WI), f32),
        rc2t=v((2, TQ, WT), f32),
        st2i=v((IQ, WI), bf16),
        st2t=v((TQ, WT), bf16),
        rx2i=v((IQ, WI), bf16),
        rx2t=v((TQ, WT), bf16),
        tb=v((TQ, WT), f32),
        tl=v((TQ, 1), f32),
        bl=v((NM, NM, IQ, IS), bf16),
        pr=v((IQ, WT), f32),
        ln=v((IQ, 1), f32),
        ei=v((NM, IQ, WT), bf16),
        et=v((NM, TQ, WT), bf16),
        cols=v((ND, TQ, WT), bf16),
        lab=v((ND, 3, 8, 128), f32),
        labo=v((8, 128), f32),
        q4t=v((TR, WT), f32),
        rc4t=v((2, TQ, WT), f32),
        st4t=v((TQ, WT), bf16),
        rx4t=v((TQ, WT), bf16),
        bfi=v((NM, IQ, WI), bf16),
        bft=v((NM, TQ, WT), bf16),
        pgf=v((IQ, WT), bf16),
        pgs=v((NM, IQ, TS), bf16),
        pgr=v((NM, IQ, TS), bf16),
        bsi=v((WI, IR), bf16),
        bst=v((WT, TR), bf16),
        an=v((3, IS, IR), bf16),
        ant=v((TS, TR), bf16),
        ab=v((3, IS, IR), bf16),
        abt=v((TS, TR), bf16),
        al=v((3, NM, IQ, IS), bf16),
        bj=v((3, NM, IQ, TS), bf16),
        ki=v((3, IR, FI), bf16),
        kt=v((TR, FT), bf16),
        g6i=v((NM, IG, IR), f32),
        g6t=v((NM, TG, TR), f32),
        rc6i=v((2, IG, IR), f32),
        rc6t=v((2, TG, TR), f32),
        st6i=v((IG, IR), bf16),
        st6t=v((TG, TR), bf16),
        rx6i=v((IG, IR), bf16),
        rx6t=v((TG, TR), bf16),
        ra1=v((2, 4 * IO, 2 * FC), bf16),
        sc1=v((4, IP, 2 * FC), bf16),
        rc1=v((4, IP, 2 * FC), bf16),
        ra2=v((4, 2 * IO, FI), bf16),
        sc2=v((2, IP, FI), bf16),
        rc2=v((2, IP, FI), bf16),
        sbj=v((2, 4 * IO, TS), bf16),
        raj=v((2, 4 * IO, TS), bf16),
        scj=v((4, IP, TS), bf16),
        rcj=v((4, IP, TS), bf16),
        sbt1=v((4, 2 * TO, FT), bf16),
        rat1=v((4, 2 * TO, FT), bf16),
        sct1=v((2, TP, FT), bf16),
        rct1=v((2, TP, FT), bf16),
        sbt2=v((4, 2 * TO, FT), bf16),
        rat2=v((4, 2 * TO, FT), bf16),
        sct2=v((2, TP, FT), bf16),
        rct2=v((2, TP, FT), bf16),
        ra1z=v((4, 2 * IO, FC), bf16),
        sc1z=v((2, IP, FC), bf16),
        rc1z=v((2, IP, FC), bf16),
        sem=pltpu.SemaphoreType.DMA((N_SEM,)),
    )


NAMES = list(scratch_list())


def step_kernel(
    img_in, txt_in, w1_in, w2_in, pj_in, tw1_in, tw2_in, label, scale, bias, loss,
    o_img, o_txt, o_w1, o_w2, o_pj, o_t1, o_t2, *scratch
):
    r = dict(zip(NAMES, scratch))
    sem = r["sem"]
    used = [0]
    t = lax.axis_index("tower")
    d = lax.axis_index("dp")
    m = lax.axis_index("mp")
    core = m % 2
    high = m // 2
    ms = m + 1 - 2 * core
    mo = (m + 2) % NM
    md = (ms + 2) % NM
    text = t == NT - 1
    image = t != NT - 1
    ti = jnp.minimum(t, 2)
    sib, opp, diag = (t, d, ms), (t, d, mo), (t, d, md)
    dy = d // 4
    dz = d % 4
    flip = (t, (d + 4) % ND, mo)
    others_t = [((t + k) % NT, d, m) for k in (1, 2, 3)]
    order_d = (4, 1, 3, 5, 7, 2, 6)
    others_d = [(d + k) % ND for k in order_d]

    def take(n):
        first = used[0]
        used[0] += n
        assert used[0] <= N_SEM
        return first

    img_sends, txt_sends, all_sends = [], [], []
    plans = []

    class Tracked:
        def __init__(self, copy, group):
            self.copy, self.group = copy, group

        def start(self):
            self.copy.start()
            self.group.append(self.copy)

    def plan(group, *steps):
        entry = {"group": group, "left": list(steps), "begun": False}
        plans.append(entry)

        def runner(step):
            def run(*args):
                entry["begun"] = True
                entry["left"].remove(step)
                return step(*args)
            return run

        return [runner(s) for s in steps]

    def send(src, dst, arrived, dev, group):
        copy = pltpu.make_async_remote_copy(
            src_ref=src, dst_ref=dst, send_sem=sem.at[take(1)], recv_sem=sem.at[arrived],
            device_id=dev, device_id_type=MESH,
        )
        return Tracked(copy, group)

    def arrive(dst, arrived):
        pltpu.make_async_remote_copy(
            src_ref=dst, dst_ref=dst, send_sem=sem.at[0], recv_sem=sem.at[arrived],
            device_id=sib, device_id_type=MESH,
        ).wait_recv()

    def gather_mp(slot, group):
        b = take(NM)
        to_opp = send(slot(m), slot(m), b + m, opp, group)
        to_sib = send(slot(m), slot(m), b + m, sib, group)
        pass_on = send(slot(mo), slot(mo), b + mo, sib, group)

        def start():
            to_opp.start()
            to_sib.start()

        def middle():
            arrive(slot(mo), b + mo)
            pass_on.start()

        def finish():
            arrive(slot(ms), b + ms)
            arrive(slot(md), b + md)

        return plan(group, start, middle, finish)

    def sum_mp(quarter, rc, st, rx, group, pack=None):
        b = take(3)
        first, second = 1 - high, high
        s1 = send(quarter(2 * first + 1 - core), rc.at[first], b + first, sib, group)
        s2 = send(quarter(2 * second + 1 - core), rc.at[second], b + second, sib, group)
        cross = send(st, rx, b + 2, opp, group)

        def start():
            s1.start()
            s2.start()

        def middle():
            arrive(rc.at[first], b + first)
            part = quarter(2 * first + core)[...] + rc[first]
            st[...] = part.astype(bf16) if pack is None else pack(part)
            cross.start()

        def finish():
            arrive(rc.at[second], b + second)
            mine = quarter(2 * second + core)[...] + rc[second]
            arrive(rx, b + 2)
            return mine

        return plan(group, start, middle, finish)

    def exchange_x(src_img, dst_img, src_txt, dst_txt):
        b = take(NT)
        ci = [send(src_img(dev[0]), dst_img(ti), b + ti, dev, img_sends) for dev in others_t]
        ct = [send(src_txt(dev[0]), dst_txt, b + 3, dev, txt_sends) for dev in others_t] if src_txt else []

        def start_img():
            for c in ci:
                c.start()

        def start_txt():
            for c in ct:
                c.start()

        def finish():
            for s in range(3):
                @pl.when(t != s)
                def _(s=s):
                    arrive(dst_img(s), b + s)
            if src_txt:
                @pl.when(image)
                def _():
                    arrive(dst_txt, b + 3)

        return plan(all_sends, start_img, start_txt, finish)

    def scatter_dp(mode, own, padded, spans, first, first_in, second, second_in):
        along_y = mode == "y"
        parts = 2 if along_y else 4
        me, rest = (dy, dz) if along_y else (dz, dy)

        def dev_first(p):
            return (t, p * 4 + dz, m) if along_y else (t, dy * 4 + p, m)

        def dev_second(p):
            return (t, dy * 4 + p, m) if along_y else (t, p * 4 + dz, m)

        steps = []
        for j, span in enumerate(spans):
            b1, b2 = take(4), take(4)
            one = [(me + k) % parts for k in range(1, parts)]
            two = [(rest + k) % (8 // parts) for k in range(1, 8 // parts)]
            c1 = [send(first(j, p), first_in.at[me, :, span], b1 + me, dev_first(p), all_sends) for p in one]
            c2 = [send(second.at[p, :, span], second_in.at[rest, :, span], b2 + rest, dev_second(p), all_sends)
                  for p in two]

            def start(c1=c1):
                for c in c1:
                    c.start()

            def middle(j=j, span=span, one=one, b1=b1, c2=c2):
                total = first(j, me)[...].astype(f32)
                for p in one:
                    arrive(first_in.at[p, :, span], b1 + p)
                    total = total + first_in[p, :, span].astype(f32)
                pad = jnp.zeros((padded - own, total.shape[1]), f32)
                for k in range(8 // parts):
                    piece = jnp.concatenate([total[k * own:(k + 1) * own], pad], axis=0)
                    second[k, :, span] = piece.astype(bf16)
                for c in c2:
                    c.start()

            def finish(out=None, at=None, span=span, two=two, b2=b2):
                total = second[rest, :, span].astype(f32)
                for p in two:
                    arrive(second_in.at[p, :, span], b2 + p)
                    total = total + second_in[p, :, span].astype(f32)
                if out is not None:
                    out[:, at or span] = total[:own]

            steps.append(plan(all_sends, start, middle, finish))
        return steps

    lb = take(5)
    mi = pl.ds(pl.multiple_of(m * IS, IS), IS)
    mt = pl.ds(pl.multiple_of(m * TS, TS), TS)
    load_xi = pltpu.make_async_copy(img_in.at[0], r["xs"].at[mi], sem.at[lb])
    load_xt = pltpu.make_async_copy(txt_in.at[0], r["xt"].at[mt], sem.at[lb + 1])
    load_w1 = pltpu.make_async_copy(w1_in, r["w1"], sem.at[lb + 2])
    load_w2 = pltpu.make_async_copy(w2_in, r["w2"], sem.at[lb + 3])
    load_pj = pltpu.make_async_copy(pj_in, r["pj"].at[mt], sem.at[lb + 4])
    tw1 = r["w1"].at[pl.ds(0, WT), pl.ds(0, FT)]
    tw2 = r["w2"].at[pl.ds(0, FT), pl.ds(0, WT)]
    load_t1 = pltpu.make_async_copy(tw1_in, tw1, sem.at[lb + 2])
    load_t2 = pltpu.make_async_copy(tw2_in, tw2, sem.at[lb + 3])

    xi_start, xi_mid, xi_fin = gather_mp(lambda i: r["xs"].at[pl.ds(pl.multiple_of(i * IS, IS), IS)], img_sends)
    xt_start, xt_mid, xt_fin = gather_mp(lambda i: r["xt"].at[pl.ds(pl.multiple_of(i * TS, TS), TS)], txt_sends)
    def head_piece(i, z):
        row = pl.multiple_of(i * TS + (z // 2) * (TS // 2), TS // 2)
        lane = pl.multiple_of((z % 2) * (WI // 2), WI // 2)
        return r["pj"].at[pl.ds(row, TS // 2), pl.ds(lane, WI // 2)]

    def head_slice(i):
        return r["pj"].at[pl.ds(pl.multiple_of(i * TS, TS), TS)]

    other_z = [(dz + k) % 4 for k in (1, 3, 2)]
    pjb, pjs, pjz = take(1), take(5), take(4)
    pj_cross = send(head_piece(m, dz), head_piece(m, dz), pjb, flip, img_sends)
    pj_own = send(head_slice(m), head_slice(m), pjs + 4, sib, img_sends)
    pj_spread = [send(head_piece(mo, dz), head_piece(mo, dz), pjz + dz, (t, dy * 4 + z, m), img_sends) for z in other_z]
    pj_pass = [send(head_piece(mo, z), head_piece(mo, z), pjs + z, sib, img_sends) for z in [dz] + other_z]

    def pj_start():
        pj_cross.start()
        pj_own.start()

    def pj_mid():
        arrive(head_piece(mo, dz), pjb)
        for c in pj_spread:
            c.start()
        pj_pass[0].start()

    def pj_fin():
        for z, c in zip(other_z, pj_pass[1:]):
            arrive(head_piece(mo, z), pjz + z)
            c.start()
        arrive(head_slice(ms), pjs + 4)
        for z in range(4):
            arrive(head_piece(md, z), pjs + z)

    pj_start, pj_mid, pj_fin = plan(img_sends, pj_start, pj_mid, pj_fin)

    lab_b = take(3)
    lab_up = send(r["labo"], r["lab"].at[d, ti], lab_b + ti, (NT - 1, d, m), img_sends)
    lab_d = take(ND)
    lab_out = [send(r["lab"].at[d], r["lab"].at[d], lab_d + d, (t, dd, m), txt_sends) for dd in others_d]

    s2i_start, s2i_mid, s2i_fin = sum_mp(lambda q: r["p2i"].at[pl.ds(q * IQ, IQ)], r["rc2i"], r["st2i"], r["rx2i"], img_sends)
    s2t_start, s2t_mid, s2t_fin = sum_mp(lambda q: r["p2t"].at[pl.ds(q * TQ, TQ)], r["rc2t"], r["st2t"], r["rx2t"], txt_sends)

    cols = r["cols"]
    star = take(3)
    star_img = send(r["ei"].at[m], cols.at[d, pl.ds(IQ * ti, IQ)], star + ti, (NT - 1, d, m), img_sends)
    star_txt = [
        send(r["et"].at[m, pl.ds(IQ * c, IQ)], cols.at[d, pl.ds(IQ * c, IQ)], star + c, dev, txt_sends)
        for c in range(3) for dev in others_t
    ]
    ring = take(3 * ND)
    ring_out = [
        [send(cols.at[d, pl.ds(IQ * c, IQ)], cols.at[d, pl.ds(IQ * c, IQ)], ring + ND * c + d, (t, dd, m), all_sends)
         for dd in others_d]
        for c in range(3)
    ]
    ei_start, ei_mid, ei_fin = gather_mp(lambda i: r["ei"].at[i], img_sends)
    et_start, et_mid, et_fin = gather_mp(lambda i: r["et"].at[i], txt_sends)
    bl_start, bl_mid, bl_fin = gather_mp(lambda i: r["bl"].at[i], img_sends)
    hid = []
    for j in range(FI // FC):
        at = slice(j * FC, (j + 1) * FC)
        hid.append(exchange_x(
            lambda s, at=at: r["hi"].at[ti, :, at], lambda s, at=at: r["hi"].at[s, :, at],
            (lambda s: r["ht"]) if j == 0 else None, r["ht"]))
    nor_si, nor_st, nor_fin = exchange_x(
        lambda s: r["ns"].at[pl.ds(s * IS, IS)], lambda s: r["an"].at[s], lambda s: r["nt"].at[pl.ds(s * TS, TS)], r["ant"])
    blx_si, _, blx_fin = exchange_x(
        lambda s: r["bl"].at[:, s], lambda s: r["al"].at[s], None, None)
    s4i_start, s4i_mid, s4i_fin = sum_mp(lambda q: r["q4t"].at[pl.ds(q * IQ, IQ)], r["rc4t"].at[:, 0:IQ], r["st4t"].at[0:IQ], r["rx4t"].at[0:IQ], img_sends)
    s4t_start, s4t_mid, s4t_fin = sum_mp(lambda q: r["q4t"].at[pl.ds(q * TQ, TQ)], r["rc4t"], r["st4t"], r["rx4t"], txt_sends)
    bi_start, bi_mid, bi_fin = gather_mp(lambda i: r["bfi"].at[i], img_sends)
    bt_start, bt_mid, bt_fin = gather_mp(lambda i: r["bft"].at[i], txt_sends)
    pgb = take(NM)
    pg_out = [
        send(r["pgs"].at[dev[2]], r["pgr"].at[m], pgb + m, dev, img_sends) for dev in (opp, diag, sib)
    ]
    pgx_si, _, pgx_fin = exchange_x(lambda s: r["pgr"], lambda s: r["bj"].at[s], None, None)
    bg_si, bg_st, bg_fin = exchange_x(
        lambda s: r["bsi"].at[pl.ds(s * IS, IS)], lambda s: r["ab"].at[s], lambda s: r["bst"].at[pl.ds(s * TS, TS)], r["abt"])
    pre = []
    for j in range(FI // FC):
        at = slice(j * FC, (j + 1) * FC)
        pre.append(exchange_x(
            lambda s, at=at: r["ki"].at[ti, :, at], lambda s, at=at: r["ki"].at[s, :, at],
            (lambda s: r["kt"]) if j == 0 else None, r["kt"]))

    def packer(width):
        def pack(part):
            sums = part[width:]
            top = sums.astype(bf16).astype(f32)
            at = lax.broadcasted_iota(jnp.int32, sums.shape, 0)
            tail = jnp.where(at == 1, sums[0:1] - top[0:1], top)
            return jnp.concatenate([part[:width], tail], axis=0).astype(bf16)
        return pack

    s6i_start, s6i_mid, s6i_fin = sum_mp(lambda q: r["g6i"].at[q], r["rc6i"], r["st6i"], r["rx6i"], img_sends, packer(IS))
    s6t_start, s6t_mid, s6t_fin = sum_mp(lambda q: r["g6t"].at[q], r["rc6t"], r["st6t"], r["rx6t"], txt_sends, packer(TS))
    spans = [slice(j * FC, (j + 1) * FC) for j in range(FI // FC)]
    whole_t = [slice(0, FT)]
    whole_j = [slice(0, TS)]
    def sb2(j, p):
        return r["w2"].at[pl.ds(pl.multiple_of(j * 8 * IO + p * 2 * IO, 2 * IO), 2 * IO), 0:FC]

    def sb1(j, p):
        return r["w1"].at[pl.ds(pl.multiple_of(p * 4 * IO, 4 * IO), 4 * IO), spans[j]]

    def sb1z(p):
        return r["w1"].at[pl.ds(pl.multiple_of(p * 2 * IO, 2 * IO), 2 * IO), spans[2]]

    w2_steps = scatter_dp(
        "z", IO, IP, spans, sb2, r["ra2"], r["sc2"], r["rc2"])
    w1_steps = scatter_dp(
        "y", IO, IP, spans[:2], sb1, r["ra1"], r["sc1"], r["rc1"])
    w1_steps += scatter_dp("z", IO, IP, [slice(0, FC)], lambda j, p: sb1z(p), r["ra1z"], r["sc1z"], r["rc1z"])
    t2_steps = scatter_dp("z", TO, TP, whole_t, lambda j, p: r["sbt2"].at[p], r["rat2"], r["sct2"], r["rct2"])
    t1_steps = scatter_dp("z", TO, TP, whole_t, lambda j, p: r["sbt1"].at[p], r["rat1"], r["sct1"], r["rct1"])
    pj_steps = scatter_dp("y", IO, IP, whole_j, lambda j, p: r["sbj"].at[p], r["raj"], r["scj"], r["rcj"])

    @pl.when(image)
    def _():
        load_xi.start()
        load_w1.start()
        load_w2.start()
        load_pj.start()

    @pl.when(text)
    def _():
        load_xt.start()
        load_t1.start()
        load_t2.start()

    barrier = pltpu.get_barrier_semaphore()
    partners = [sib, opp, diag, flip] + others_t + [(t, dd, m) for dd in others_d]
    for dev in partners:
        pl.semaphore_signal(barrier, inc=1, device_id=dev, device_id_type=MESH)
    pl.semaphore_wait(barrier, len(partners))

    @pl.when(image)
    def _():
        load_xi.wait()
        xi_start()
        r["labo"][...] = jnp.full((8, 128), label[0, 0].astype(f32))
        lab_up.start()
        load_pj.wait()
        pj_start()
        xi_mid()
        xi_fin()
        xt32 = r["xs"][...].astype(f32)
        inv = lax.rsqrt(jnp.sum(xt32 * xt32, axis=0, keepdims=True) / WI + epsilon)
        r["ivi"][...] = inv
        r["ns"][...] = (xt32 * inv).astype(bf16)
        nor_si()
        r["nf"][...] = r["ns"][...].T

    @pl.when(text)
    def _():
        load_xt.wait()
        xt_start()
        xt_mid()
        xt_fin()
        xt32 = r["xt"][...].astype(f32)
        inv = lax.rsqrt(jnp.sum(xt32 * xt32, axis=0, keepdims=True) / WT + epsilon)
        r["ivt"][...] = inv
        r["nt"][...] = (xt32 * inv).astype(bf16)
        nor_st()
        r["ntf"][...] = r["nt"][...].T

    @pl.when(image)
    def _():
        load_w1.wait()

        def front(j, carry):
            at = pl.ds(pl.multiple_of(j * 384, 384), 384)
            u = dot(r["nf"][...], r["w1"][:, at])
            val, slope = gelu_both(u)
            r["hi"][ti, :, at] = val.astype(bf16)
            r["gi"][:, at] = slope
            return carry

        lax.fori_loop(0, FI // 384, front, 0)

    @pl.when(text)
    def _():
        load_t1.wait()

        for at in (slice(0, 256), slice(256, 512), slice(512, 640)):
            val, slope = gelu_both(dot(r["ntf"][...], r["w1"][0:WT, at]))
            r["ht"][:, at] = val.astype(bf16)
            r["gt"][:, at] = slope

    @pl.when(image)
    def _():
        hid[0][0]()
        hid[1][0]()
        load_w2.wait()

        def back(j, carry):
            at = pl.ds(pl.multiple_of(j * 256, 256), 256)
            r["p2i"][:, at] = dot(r["hi"][ti], r["w2"][:, at])
            return carry

        lax.fori_loop(0, WI // 256, back, 0)

    @pl.when(text)
    def _():
        load_t2.wait()

        def back(j, carry):
            at = pl.ds(pl.multiple_of(j * 384, 384), 384)
            r["p2t"][:, at] = dot(r["ht"][...], r["w2"][0:FT, at])
            return carry

        lax.fori_loop(0, WT // 384, back, 0)
        for s in range(3):
            arrive(r["lab"].at[d, s], lab_b + s)
        for c in lab_out:
            c.start()

    @pl.when(image)
    def _():
        s2i_start()
        pj_mid()
        r["xf"][...] = r["xs"][...].T
        s2i_mid()
        part = s2i_fin()
        rows = pl.ds(pl.multiple_of(m * IQ, IQ), IQ)
        x = r["xf"][rows, :].astype(f32)
        blended = (x + (part + r["rx2i"][...].astype(f32))).astype(bf16)
        for k in range(NM):
            r["bl"][m, k] = blended[:, k * IS:(k + 1) * IS]
        pj_fin()
        projected = dot_t(blended, r["pj"][...])
        length = jnp.sqrt(jnp.sum(projected * projected, axis=1, keepdims=True))
        r["pr"][...] = projected
        r["ln"][...] = length
        r["ei"][m] = (projected / length).astype(bf16)
        star_img.start()
        ei_start()
        bl_start()

    @pl.when(text)
    def _():
        s2t_start()
        r["xtf"][...] = r["xt"][...].T
        s2t_mid()
        part = s2t_fin()
        rows = pl.ds(pl.multiple_of(m * TQ, TQ), TQ)
        x = r["xtf"][rows, :].astype(f32)
        blended = x + (part + r["rx2t"][...].astype(f32))
        length = jnp.sqrt(jnp.sum(blended * blended, axis=1, keepdims=True))
        r["tb"][...] = blended
        r["tl"][...] = length
        r["et"][m] = (blended / length).astype(bf16)
        for c in star_txt:
            c.start()
        et_start()

    for c in range(3):
        arrive(cols.at[d, pl.ds(IQ * c, IQ)], star + c)
        for copy in ring_out[c]:
            copy.start()

    @pl.when(image)
    def _():
        ei_mid()
        hid[2][0]()
        bl_mid()
        ei_fin()

    @pl.when(text)
    def _():
        et_mid()
        hid[0][1]()
        et_fin()
        for dd in others_d:
            arrive(r["lab"].at[dd], lab_d + dd)

    scale_v, bias_v, loss_v = scale[0, 0], bias[0, 0], loss[0, 0]

    def weight(scores, positive):
        logits = scale_v * scores + bias_v
        signed = jnp.where(positive, 1.0, -1.0).astype(f32)
        grad = -loss_v * signed * jax.nn.sigmoid(-signed * logits)
        return (scale_v * grad).astype(bf16)

    def block_ready(dd):
        for c in range(3):
            arrive(cols.at[dd, pl.ds(IQ * c, IQ)], ring + ND * c + dd)

    @pl.when(image)
    def _():
        emb = r["ei"][...].reshape(IR, WT)
        row = (t * ND + d) * IR + lax.broadcasted_iota(jnp.int32, (IR, TQ), 0) + label[0, 0]
        target = jnp.where(row >= BATCH, row - BATCH, row)
        lane = lax.broadcasted_iota(jnp.int32, (IR, TQ), 1)

        def block(dd):
            pw = weight(dot_t(emb, cols[dd]), target == lane + (dd * TR + m * TQ))
            return dot(pw, cols[dd])

        r["q4t"][0:IR] = block(d)

        def step(k, carry):
            dd = (d + k) % ND
            block_ready(dd)
            r["q4t"][0:IR] += block(dd)
            return carry

        lax.fori_loop(1, ND, step, 0)

    @pl.when(text)
    def _():
        emb = r["et"][...].reshape(TR, WT)
        row = d * TR + lax.broadcasted_iota(jnp.int32, (TR, TQ), 0)
        lane = lax.broadcasted_iota(jnp.int32, (1, TQ), 1)
        part = lane // IQ

        def block(dd):
            off = r["lab"][dd]
            off = jnp.where(part == 0, off[0, :1, :TQ], jnp.where(part == 1, off[1, :1, :TQ], off[2, :1, :TQ]))
            own = (part * ND + dd) * IR + m * IQ + lane % IQ
            target = own + off.astype(jnp.int32)
            target = jnp.where(target >= BATCH, target - BATCH, target)
            pw = weight(dot_t(emb, cols[dd]), row == target)
            return dot(pw, cols[dd])

        r["q4t"][...] = block(d)

        def step(k, carry):
            dd = (d + k) % ND
            block_ready(dd)
            r["q4t"][...] += block(dd)
            return carry

        lax.fori_loop(1, ND, step, 0)

    @pl.when(image)
    def _():
        s4i_start()
        s4i_mid()
        part = s4i_fin()
        grad = part + r["rx4t"][0:IQ].astype(f32)
        length = r["ln"][...]
        direction = r["pr"][...] / length
        pg = ((grad - direction * jnp.sum(direction * grad, axis=1, keepdims=True)) / length).astype(bf16)
        r["bfi"][m] = dot(pg, r["pj"][...]).astype(bf16)
        r["pgf"][...] = pg

    @pl.when(text)
    def _():
        s4t_start()
        s4t_mid()
        part = s4t_fin()
        grad = part + r["rx4t"][...].astype(f32)
        length = r["tl"][...]
        direction = r["tb"][...] / length
        blended_grad = (grad - direction * jnp.sum(direction * grad, axis=1, keepdims=True)) / length
        r["bft"][m] = blended_grad.astype(bf16)

    @pl.when(image)
    def _():
        bi_start()
        for k in range(NM):
            r["pgs"][k] = r["pgf"][:, k * TS:(k + 1) * TS]
        r["pgr"][m] = r["pgs"][m]
        for c in pg_out:
            c.start()
        bl_fin()
        blx_si()
        r["al"][ti] = r["bl"][:, ti]
        r["an"][ti] = r["ns"][pl.ds(pl.multiple_of(ti * IS, IS), IS), :]
        bi_mid()
        bi_fin()
        r["bsi"][...] = r["bfi"][...].reshape(IR, WI).T
        bg_si()
        r["ab"][ti] = r["bsi"][pl.ds(pl.multiple_of(ti * IS, IS), IS), :]

    @pl.when(text)
    def _():
        bt_start()
        r["ant"][...] = r["nt"][(NT - 1) * TS:]
        bt_mid()
        bt_fin()
        r["bst"][...] = r["bft"][...].reshape(TR, WT).T
        bg_st()
        r["abt"][...] = r["bst"][(NT - 1) * TS:]

    @pl.when(image)
    def _():
        for j in range(FI // FC):
            for lo, wide in ((0, 384), (384, 256)):
                at = slice(j * FC + lo, j * FC + lo + wide)
                hg = dot_t(r["bfi"][...].reshape(IR, WI), r["w2"][at, :])
                r["ki"][ti, :, at] = (hg * r["gi"][:, at]).astype(bf16)
            if j == 0:
                pre[0][0]()
        for dev in (opp, diag, sib):
            arrive(r["pgr"].at[dev[2]], pgb + dev[2])
        pgx_si()
        r["bj"][ti] = r["pgr"][...]

    @pl.when(text)
    def _():
        for at in (slice(0, 384), slice(384, 640)):
            hg = dot_t(r["bft"][...].reshape(TR, WT), r["w2"][at, 0:WT])
            r["kt"][:, at] = (hg * r["gt"][:, at]).astype(bf16)
        pre[0][1]()

    def by_z(g, own, dst, at):
        for p in range(4):
            pair = [g[(q * 4 + p) * own:(q * 4 + p + 1) * own] for q in range(2)]
            dst(p)[:, at] = jnp.concatenate(pair, axis=0).astype(bf16)

    def by_y(g, own, dst, at):
        for p in range(2):
            dst(p)[:, at] = g[p * 4 * own:(p + 1) * 4 * own].astype(bf16)

    def product(lhs, rhs, put, own, dst, begin, width):
        done = 0
        while done < width:
            wide = min(384, width - done)
            put(dot(lhs, rhs(slice(begin + done, begin + done + wide))), own, dst, slice(done, done + wide))
            done += wide

    def three(name):
        return jnp.concatenate([r[name][s] for s in range(3)], axis=1)

    bg_fin()
    for j in range(FI // FC):
        hid[j][2]()
        product(three("ab"), lambda at: r["hi"][:, :, at].reshape(3 * IR, at.stop - at.start),
                by_z, IO, lambda p, j=j: sb2(j, p), j * FC, FC)
        w2_steps[j][0]()
        if j == 1:
            @pl.when(image)
            def _():
                pre[1][0]()
    product(r["abt"][...], lambda at: r["ht"][:, at], by_z, TO, lambda p: r["sbt2"].at[p], 0, FT)
    t2_steps[0][0]()

    @pl.when(image)
    def _():
        total = jnp.zeros((1, IR), f32)
        for k in range(NM):
            g = dot_t(r["w1"][k * IS:(k + 1) * IS, :], r["ki"][ti])
            total = total + jnp.sum(r["ns"][k * IS:(k + 1) * IS, :].astype(f32) * g, axis=0, keepdims=True)
            r["g6i"][k, 0:IS, :] = g
        tail = jnp.broadcast_to(total, (16, IR))
        for k in range(NM):
            r["g6i"][k, IS:IG, :] = tail
        s6i_start()
        pre[2][0]()

    @pl.when(text)
    def _():
        total = jnp.zeros((1, TR), f32)
        for k in range(NM):
            g = dot_t(r["w1"][k * TS:(k + 1) * TS, 0:FT], r["kt"][...])
            total = total + jnp.sum(r["nt"][k * TS:(k + 1) * TS, :].astype(f32) * g, axis=0, keepdims=True)
            r["g6t"][k, 0:TS, :] = g
        tail = jnp.broadcast_to(total, (16, TR))
        for k in range(NM):
            r["g6t"][k, TS:TG, :] = tail
        s6t_start()

    blx_fin()
    pgx_fin()
    by_y(dot_rows(r["al"][...].reshape(3 * IR, IS), r["bj"][...].reshape(3 * IR, TS)), IO,
         lambda p: r["sbj"].at[p], slice(0, TS))
    pj_steps[0][0]()
    nor_fin()
    for j in range(FI // FC):
        pre[j][2]()
        product(three("an"), lambda at: r["ki"][:, :, at].reshape(3 * IR, at.stop - at.start),
                by_z if j == 2 else by_y, IO, (lambda p: sb1z(p)) if j == 2 else (lambda p, j=j: sb1(j, p)), j * FC, FC)
        w1_steps[j][0]()
        if j == 0:
            @pl.when(image)
            def _():
                s6i_mid()

            @pl.when(text)
            def _():
                s6t_mid()
            product(r["ant"][...], lambda at: r["kt"][:, at], by_z, TO, lambda p: r["sbt1"].at[p], 0, FT)
            t1_steps[0][0]()
        w2_steps[j][1]()
        if j == 1:
            t2_steps[0][1]()
            w1_steps[0][1]()
    w1_steps[1][1]()
    pj_steps[0][1]()

    @pl.when(image)
    def _():
        part = s6i_fin()
        other = r["rx6i"][...].astype(f32)
        average = (part[IS:IS + 1] + other[IS:IS + 1] + other[IS + 1:IS + 2]) / WI
        grad = part[:IS] + other[:IS]
        inv = r["ivi"][...]
        normed = r["xs"][mi, :].astype(f32) * inv
        o_img[0] = r["bsi"][mi, :].astype(f32) + (grad - normed * average) * inv
        o_txt[0] = jnp.zeros((TS, TR), f32)

    @pl.when(text)
    def _():
        part = s6t_fin()
        other = r["rx6t"][...].astype(f32)
        average = (part[TS:TS + 1] + other[TS:TS + 1] + other[TS + 1:TS + 2]) / WT
        grad = part[:TS] + other[:TS]
        inv = r["ivt"][...]
        normed = r["xt"][mt, :].astype(f32) * inv
        o_txt[0] = r["bst"][mt, :].astype(f32) + (grad - normed * average) * inv
        o_img[0] = jnp.zeros((IS, IR), f32)

    w1_steps[2][1]()
    t1_steps[0][1]()
    for j in range(FI // FC):
        w2_steps[j][2](o_w2)
    t2_steps[0][2](o_t2)
    pj_steps[0][2](o_pj)
    for j in range(FI // FC):
        w1_steps[j][2](o_w1, spans[j])
    t1_steps[0][2](o_t1)

    for c in all_sends:
        c.wait_send()

    @pl.when(image)
    def _():
        for c in img_sends:
            c.wait_send()

    @pl.when(text)
    def _():
        for c in txt_sends:
            c.wait_send()


def move(*refs):
    n = len(refs) // 2
    sem = refs[-1]
    copies = [pltpu.make_async_copy(refs[k], refs[n + k], sem.at[k]) for k in range(n)]
    for c in copies:
        c.start()
    for c in copies:
        c.wait()


def per_device(
    image_in, text_in, img_w1, img_w2, img_proj, txt_w1, txt_w2, label_offset,
    logit_scale, logit_bias, loss_scale,
):
    anywhere = pl.BlockSpec(memory_space=pl.ANY)
    scalar = pl.BlockSpec(memory_space=pltpu.SMEM)
    vmem = pl.BlockSpec(memory_space=pltpu.VMEM)
    one = lambda v: v.reshape(1, 1)
    outs = pl.pallas_call(
        step_kernel,
        out_shape=[
            jax.ShapeDtypeStruct((1, IS, IR), f32),
            jax.ShapeDtypeStruct((1, TS, TR), f32),
            jax.ShapeDtypeStruct((IO, FI), f32),
            jax.ShapeDtypeStruct((IO, FI), f32),
            jax.ShapeDtypeStruct((IO, TS), f32),
            jax.ShapeDtypeStruct((TO, FT), f32),
            jax.ShapeDtypeStruct((TO, FT), f32),
        ],
        in_specs=[anywhere] * 7 + [scalar] * 4,
        out_specs=[vmem] * 7,
        scratch_shapes=list(scratch_list().values()),
        compiler_params=pltpu.CompilerParams(
            collective_id=0, has_side_effects=True, vmem_limit_bytes=63 << 20
        ),
        name="step",
    )(
        image_in.swapaxes(1, 2), text_in.swapaxes(1, 2), img_w1, img_w2, img_proj.T, txt_w1, txt_w2, label_offset,
        one(logit_scale), one(logit_bias), one(loss_scale),
    )
    outs = pl.pallas_call(
        move,
        out_shape=[jax.ShapeDtypeStruct(o.shape, o.dtype) for o in outs],
        in_specs=[anywhere] * len(outs),
        out_specs=[vmem] * len(outs),
        scratch_shapes=[pltpu.SemaphoreType.DMA((len(outs),))],
        name="place",
    )(*outs)
    g_img, g_txt, g_w1, g_w2, g_pj, g_t1, g_t2 = outs
    return (g_img.swapaxes(1, 2), g_txt.swapaxes(1, 2), g_w1, g_w2.T, g_pj, g_t1, g_t2.T)


def solution(mesh):
    return jax.shard_map(
        per_device,
        mesh=mesh,
        in_specs=(
            P("tower", "dp", "mp"),
            P("tower", "dp", "mp"),
            P(None, "mp"),
            P("mp", None),
            P(None, "mp"),
            P(None, "mp"),
            P("mp", None),
            P("tower", "dp"),
            P(),
            P(),
            P(),
        ),
        out_specs=(
            P("tower", "dp", "mp"),
            P("tower", "dp", "mp"),
            P(("tower", "dp"), "mp"),
            P("mp", ("tower", "dp")),
            P(("tower", "dp"), "mp"),
            P(("tower", "dp"), "mp"),
            P("mp", ("tower", "dp")),
        ),
        check_vma=False,
    )
```

```python
import functools
import math

import jax
import jax.numpy as jnp
from jax import lax
from jax.experimental import pallas as pl
from jax.experimental.pallas import tpu as pltpu
from jax.sharding import PartitionSpec as P

epsilon = 1e-06
bf16 = jnp.bfloat16
f32 = jnp.float32
MESH = pl.DeviceIdType.MESH
GELU_A = math.sqrt(2.0 / math.pi)
GELU_B = 0.044715

NT = 4
ND = 8
NM = 4
IR = 128
TR = 384
IQ = IR // NM
TQ = TR // NM
WI = 1792
WT = 1152
IS = WI // NM
TS = WT // NM
FI = 1920
FT = 640
BATCH = 3072
IO = WI // 32
TO = WT // 32
IP = 64
TP = 48
IG = IS + 16
TG = TS + 16
FC = 640
N_SEM = 420
LIMIT = None


def dot(a, b):
    return jnp.dot(a, b, preferred_element_type=f32)


def dot_t(a, b):
    return lax.dot_general(a, b, (((1,), (1,)), ((), ())), preferred_element_type=f32)


def dot_rows(a, b):
    return lax.dot_general(a, b, (((0,), (0,)), ((), ())), preferred_element_type=f32)


def gelu_both(u):
    sq = u * u
    th = jnp.tanh(GELU_A * u * (1.0 + GELU_B * sq))
    half = 0.5 * (1.0 + th)
    slope = half + 0.5 * u * (1.0 - th * th) * (GELU_A * (1.0 + 3.0 * GELU_B * sq))
    return u * half, slope


def scratch_list():
    v = pltpu.VMEM
    return dict(
        w1=v((WI, FI), bf16),
        w2=v((FI, WI), bf16),
        pj=v((WT, WI), bf16),
        xs=v((WI, IR), bf16),
        xt=v((WT, TR), bf16),
        xf=v((IR, WI), bf16),
        xtf=v((TR, WT), bf16),
        ns=v((WI, IR), bf16),
        nt=v((WT, TR), bf16),
        nf=v((IR, WI), bf16),
        ntf=v((TR, WT), bf16),
        ivi=v((1, IR), f32),
        ivt=v((1, TR), f32),
        hi=v((3, IR, FI), bf16),
        ht=v((TR, FT), bf16),
        gi=v((IR, FI), f32),
        gt=v((TR, FT), f32),
        p2i=v((IR, WI), f32),
        p2t=v((TR, WT), f32),
        rc2i=v((2, IQ, WI), f32),
        rc2t=v((2, TQ, WT), f32),
        st2i=v((IQ, WI), bf16),
        st2t=v((TQ, WT), bf16),
        rx2i=v((IQ, WI), bf16),
        rx2t=v((TQ, WT), bf16),
        tb=v((TQ, WT), f32),
        tl=v((TQ, 1), f32),
        bl=v((NM, NM, IQ, IS), bf16),
        pr=v((IQ, WT), f32),
        ln=v((IQ, 1), f32),
        ei=v((NM, IQ, WT), bf16),
        et=v((NM, TQ, WT), bf16),
        cols=v((ND, TQ, WT), bf16),
        lab=v((ND, 3, 8, 128), f32),
        labo=v((8, 128), f32),
        q4t=v((TR, WT), f32),
        rc4t=v((2, TQ, WT), f32),
        st4t=v((TQ, WT), bf16),
        rx4t=v((TQ, WT), bf16),
        bfi=v((NM, IQ, WI), bf16),
        bft=v((NM, TQ, WT), bf16),
        pgf=v((IQ, WT), bf16),
        pgs=v((NM, IQ, TS), bf16),
        pgr=v((NM, IQ, TS), bf16),
        bsi=v((WI, IR), bf16),
        bst=v((WT, TR), bf16),
        an=v((3, IS, IR), bf16),
        ant=v((TS, TR), bf16),
        ab=v((3, IS, IR), bf16),
        abt=v((TS, TR), bf16),
        al=v((3, NM, IQ, IS), bf16),
        bj=v((3, NM, IQ, TS), bf16),
        ki=v((3, IR, FI), bf16),
        kt=v((TR, FT), bf16),
        g6i=v((NM, IG, IR), f32),
        g6t=v((NM, TG, TR), f32),
        rc6i=v((2, IG, IR), f32),
        rc6t=v((2, TG, TR), f32),
        st6i=v((IG, IR), bf16),
        st6t=v((TG, TR), bf16),
        rx6i=v((IG, IR), bf16),
        rx6t=v((TG, TR), bf16),
        ra1=v((2, 4 * IO, 2 * FC), bf16),
        sc1=v((4, IP, 2 * FC), bf16),
        rc1=v((4, IP, 2 * FC), bf16),
        ra2=v((4, 2 * IO, FI), bf16),
        sc2=v((2, IP, FI), bf16),
        rc2=v((2, IP, FI), bf16),
        sbj=v((2, 4 * IO, TS), bf16),
        raj=v((2, 4 * IO, TS), bf16),
        scj=v((4, IP, TS), bf16),
        rcj=v((4, IP, TS), bf16),
        sbt1=v((4, 2 * TO, FT), bf16),
        rat1=v((4, 2 * TO, FT), bf16),
        sct1=v((2, TP, FT), bf16),
        rct1=v((2, TP, FT), bf16),
        sbt2=v((4, 2 * TO, FT), bf16),
        rat2=v((4, 2 * TO, FT), bf16),
        sct2=v((2, TP, FT), bf16),
        rct2=v((2, TP, FT), bf16),
        ra1z=v((4, 2 * IO, FC), bf16),
        sc1z=v((2, IP, FC), bf16),
        rc1z=v((2, IP, FC), bf16),
        sem=pltpu.SemaphoreType.DMA((N_SEM,)),
    )


NAMES = list(scratch_list())


def step_kernel(
    img_in, txt_in, w1_in, w2_in, pj_in, tw1_in, tw2_in, label, scale, bias, loss,
    o_img, o_txt, o_w1, o_w2, o_pj, o_t1, o_t2, *scratch
):
    r = dict(zip(NAMES, scratch))
    sem = r["sem"]
    used = [0]
    t = lax.axis_index("tower")
    d = lax.axis_index("dp")
    m = lax.axis_index("mp")
    core = m % 2
    high = m // 2
    ms = m + 1 - 2 * core
    mo = (m + 2) % NM
    md = (ms + 2) % NM
    text = t == NT - 1
    image = t != NT - 1
    ti = jnp.minimum(t, 2)
    sib, opp, diag = (t, d, ms), (t, d, mo), (t, d, md)
    dy = d // 4
    dz = d % 4
    flip = (t, (d + 4) % ND, mo)
    others_t = [((t + k) % NT, d, m) for k in (1, 2, 3)]
    order_d = (4, 1, 3, 5, 7, 2, 6)
    others_d = [(d + k) % ND for k in order_d]

    def take(n):
        first = used[0]
        used[0] += n
        assert used[0] <= N_SEM
        return first

    img_sends, txt_sends, all_sends = [], [], []
    plans = []

    class Tracked:
        def __init__(self, copy, group):
            self.copy, self.group = copy, group

        def start(self):
            self.copy.start()
            self.group.append(self.copy)

    def plan(group, *steps):
        entry = {"group": group, "left": list(steps), "begun": False}
        plans.append(entry)

        def runner(step):
            def run(*args):
                entry["begun"] = True
                entry["left"].remove(step)
                return step(*args)
            return run

        return [runner(s) for s in steps]

    def send(src, dst, arrived, dev, group):
        copy = pltpu.make_async_remote_copy(
            src_ref=src, dst_ref=dst, send_sem=sem.at[take(1)], recv_sem=sem.at[arrived],
            device_id=dev, device_id_type=MESH,
        )
        return Tracked(copy, group)

    def arrive(dst, arrived):
        pltpu.make_async_remote_copy(
            src_ref=dst, dst_ref=dst, send_sem=sem.at[0], recv_sem=sem.at[arrived],
            device_id=sib, device_id_type=MESH,
        ).wait_recv()

    def gather_mp(slot, group):
        b = take(NM)
        to_opp = send(slot(m), slot(m), b + m, opp, group)
        to_sib = send(slot(m), slot(m), b + m, sib, group)
        pass_on = send(slot(mo), slot(mo), b + mo, sib, group)

        def start():
            to_opp.start()
            to_sib.start()

        def middle():
            arrive(slot(mo), b + mo)
            pass_on.start()

        def finish():
            arrive(slot(ms), b + ms)
            arrive(slot(md), b + md)

        return plan(group, start, middle, finish)

    def sum_mp(quarter, rc, st, rx, group, pack=None):
        b = take(3)
        first, second = 1 - high, high
        s1 = send(quarter(2 * first + 1 - core), rc.at[first], b + first, sib, group)
        s2 = send(quarter(2 * second + 1 - core), rc.at[second], b + second, sib, group)
        cross = send(st, rx, b + 2, opp, group)

        def start():
            s1.start()
            s2.start()

        def middle():
            arrive(rc.at[first], b + first)
            part = quarter(2 * first + core)[...] + rc[first]
            st[...] = part.astype(bf16) if pack is None else pack(part)
            cross.start()

        def finish():
            arrive(rc.at[second], b + second)
            mine = quarter(2 * second + core)[...] + rc[second]
            arrive(rx, b + 2)
            return mine

        return plan(group, start, middle, finish)

    def exchange_x(src_img, dst_img, src_txt, dst_txt):
        b = take(NT)
        ci = [send(src_img(dev[0]), dst_img(ti), b + ti, dev, img_sends) for dev in others_t]
        ct = [send(src_txt(dev[0]), dst_txt, b + 3, dev, txt_sends) for dev in others_t] if src_txt else []

        def start_img():
            for c in ci:
                c.start()

        def start_txt():
            for c in ct:
                c.start()

        def finish():
            for s in range(3):
                @pl.when(t != s)
                def _(s=s):
                    arrive(dst_img(s), b + s)
            if src_txt:
                @pl.when(image)
                def _():
                    arrive(dst_txt, b + 3)

        return plan(all_sends, start_img, start_txt, finish)

    def scatter_dp(mode, own, padded, spans, first, first_in, second, second_in):
        along_y = mode == "y"
        parts = 2 if along_y else 4
        me, rest = (dy, dz) if along_y else (dz, dy)

        def dev_first(p):
            return (t, p * 4 + dz, m) if along_y else (t, dy * 4 + p, m)

        def dev_second(p):
            return (t, dy * 4 + p, m) if along_y else (t, p * 4 + dz, m)

        steps = []
        for j, span in enumerate(spans):
            b1, b2 = take(4), take(4)
            one = [(me + k) % parts for k in range(1, parts)]
            two = [(rest + k) % (8 // parts) for k in range(1, 8 // parts)]
            c1 = [send(first(j, p), first_in.at[me, :, span], b1 + me, dev_first(p), all_sends) for p in one]
            c2 = [send(second.at[p, :, span], second_in.at[rest, :, span], b2 + rest, dev_second(p), all_sends)
                  for p in two]

            def start(c1=c1):
                for c in c1:
                    c.start()

            def middle(j=j, span=span, one=one, b1=b1, c2=c2):
                total = first(j, me)[...].astype(f32)
                for p in one:
                    arrive(first_in.at[p, :, span], b1 + p)
                    total = total + first_in[p, :, span].astype(f32)
                pad = jnp.zeros((padded - own, total.shape[1]), f32)
                for k in range(8 // parts):
                    piece = jnp.concatenate([total[k * own:(k + 1) * own], pad], axis=0)
                    second[k, :, span] = piece.astype(bf16)
                for c in c2:
                    c.start()

            def finish(out=None, at=None, span=span, two=two, b2=b2):
                total = second[rest, :, span].astype(f32)
                for p in two:
                    arrive(second_in.at[p, :, span], b2 + p)
                    total = total + second_in[p, :, span].astype(f32)
                if out is not None:
                    out[:, at or span] = total[:own]

            steps.append(plan(all_sends, start, middle, finish))
        return steps

    lb = take(5)
    mi = pl.ds(pl.multiple_of(m * IS, IS), IS)
    mt = pl.ds(pl.multiple_of(m * TS, TS), TS)
    load_xi = pltpu.make_async_copy(img_in.at[0], r["xs"].at[mi], sem.at[lb])
    load_xt = pltpu.make_async_copy(txt_in.at[0], r["xt"].at[mt], sem.at[lb + 1])
    load_w1 = pltpu.make_async_copy(w1_in, r["w1"], sem.at[lb + 2])
    load_w2 = pltpu.make_async_copy(w2_in, r["w2"], sem.at[lb + 3])
    load_pj = pltpu.make_async_copy(pj_in, r["pj"].at[mt], sem.at[lb + 4])
    tw1 = r["w1"].at[pl.ds(0, WT), pl.ds(0, FT)]
    tw2 = r["w2"].at[pl.ds(0, FT), pl.ds(0, WT)]
    load_t1 = pltpu.make_async_copy(tw1_in, tw1, sem.at[lb + 2])
    load_t2 = pltpu.make_async_copy(tw2_in, tw2, sem.at[lb + 3])

    xi_start, xi_mid, xi_fin = gather_mp(lambda i: r["xs"].at[pl.ds(pl.multiple_of(i * IS, IS), IS)], img_sends)
    xt_start, xt_mid, xt_fin = gather_mp(lambda i: r["xt"].at[pl.ds(pl.multiple_of(i * TS, TS), TS)], txt_sends)
    def head_piece(i, z):
        row = pl.multiple_of(i * TS + (z // 2) * (TS // 2), TS // 2)
        lane = pl.multiple_of((z % 2) * (WI // 2), WI // 2)
        return r["pj"].at[pl.ds(row, TS // 2), pl.ds(lane, WI // 2)]

    def head_slice(i):
        return r["pj"].at[pl.ds(pl.multiple_of(i * TS, TS), TS)]

    other_z = [(dz + k) % 4 for k in (1, 3, 2)]
    pjb, pjs, pjz = take(1), take(5), take(4)
    pj_cross = send(head_piece(m, dz), head_piece(m, dz), pjb, flip, img_sends)
    pj_own = send(head_slice(m), head_slice(m), pjs + 4, sib, img_sends)
    pj_spread = [send(head_piece(mo, dz), head_piece(mo, dz), pjz + dz, (t, dy * 4 + z, m), img_sends) for z in other_z]
    pj_pass = [send(head_piece(mo, z), head_piece(mo, z), pjs + z, sib, img_sends) for z in [dz] + other_z]

    def pj_start():
        pj_cross.start()
        pj_own.start()

    def pj_mid():
        arrive(head_piece(mo, dz), pjb)
        for c in pj_spread:
            c.start()
        pj_pass[0].start()

    def pj_fin():
        for z, c in zip(other_z, pj_pass[1:]):
            arrive(head_piece(mo, z), pjz + z)
            c.start()
        arrive(head_slice(ms), pjs + 4)
        for z in range(4):
            arrive(head_piece(md, z), pjs + z)

    pj_start, pj_mid, pj_fin = plan(img_sends, pj_start, pj_mid, pj_fin)

    lab_b = take(3)
    lab_up = send(r["labo"], r["lab"].at[d, ti], lab_b + ti, (NT - 1, d, m), img_sends)
    lab_d = take(ND)
    lab_out = [send(r["lab"].at[d], r["lab"].at[d], lab_d + d, (t, dd, m), txt_sends) for dd in others_d]

    s2i_start, s2i_mid, s2i_fin = sum_mp(lambda q: r["p2i"].at[pl.ds(q * IQ, IQ)], r["rc2i"], r["st2i"], r["rx2i"], img_sends)
    s2t_start, s2t_mid, s2t_fin = sum_mp(lambda q: r["p2t"].at[pl.ds(q * TQ, TQ)], r["rc2t"], r["st2t"], r["rx2t"], txt_sends)

    cols = r["cols"]
    star = take(3)
    star_img = send(r["ei"].at[m], cols.at[d, pl.ds(IQ * ti, IQ)], star + ti, (NT - 1, d, m), img_sends)
    star_txt = [
        send(r["et"].at[m, pl.ds(IQ * c, IQ)], cols.at[d, pl.ds(IQ * c, IQ)], star + c, dev, txt_sends)
        for c in range(3) for dev in others_t
    ]
    ring = take(3 * ND)
    ring_out = [
        [send(cols.at[d, pl.ds(IQ * c, IQ)], cols.at[d, pl.ds(IQ * c, IQ)], ring + ND * c + d, (t, dd, m), all_sends)
         for dd in others_d]
        for c in range(3)
    ]
    ei_start, ei_mid, ei_fin = gather_mp(lambda i: r["ei"].at[i], img_sends)
    et_start, et_mid, et_fin = gather_mp(lambda i: r["et"].at[i], txt_sends)
    bl_start, bl_mid, bl_fin = gather_mp(lambda i: r["bl"].at[i], img_sends)
    hid = []
    for j in range(FI // FC):
        at = slice(j * FC, (j + 1) * FC)
        hid.append(exchange_x(
            lambda s, at=at: r["hi"].at[ti, :, at], lambda s, at=at: r["hi"].at[s, :, at],
            (lambda s: r["ht"]) if j == 0 else None, r["ht"]))
    nor_si, nor_st, nor_fin = exchange_x(
        lambda s: r["ns"].at[pl.ds(s * IS, IS)], lambda s: r["an"].at[s], lambda s: r["nt"].at[pl.ds(s * TS, TS)], r["ant"])
    blx_si, _, blx_fin = exchange_x(
        lambda s: r["bl"].at[:, s], lambda s: r["al"].at[s], None, None)
    s4i_start, s4i_mid, s4i_fin = sum_mp(lambda q: r["q4t"].at[pl.ds(q * IQ, IQ)], r["rc4t"].at[:, 0:IQ], r["st4t"].at[0:IQ], r["rx4t"].at[0:IQ], img_sends)
    s4t_start, s4t_mid, s4t_fin = sum_mp(lambda q: r["q4t"].at[pl.ds(q * TQ, TQ)], r["rc4t"], r["st4t"], r["rx4t"], txt_sends)
    bi_start, bi_mid, bi_fin = gather_mp(lambda i: r["bfi"].at[i], img_sends)
    bt_start, bt_mid, bt_fin = gather_mp(lambda i: r["bft"].at[i], txt_sends)
    pgb = take(NM)
    pg_out = [
        send(r["pgs"].at[dev[2]], r["pgr"].at[m], pgb + m, dev, img_sends) for dev in (opp, diag, sib)
    ]
    pgx_si, _, pgx_fin = exchange_x(lambda s: r["pgr"], lambda s: r["bj"].at[s], None, None)
    bg_si, bg_st, bg_fin = exchange_x(
        lambda s: r["bsi"].at[pl.ds(s * IS, IS)], lambda s: r["ab"].at[s], lambda s: r["bst"].at[pl.ds(s * TS, TS)], r["abt"])
    pre = []
    for j in range(FI // FC):
        at = slice(j * FC, (j + 1) * FC)
        pre.append(exchange_x(
            lambda s, at=at: r["ki"].at[ti, :, at], lambda s, at=at: r["ki"].at[s, :, at],
            (lambda s: r["kt"]) if j == 0 else None, r["kt"]))

    def packer(width):
        def pack(part):
            sums = part[width:]
            top = sums.astype(bf16).astype(f32)
            at = lax.broadcasted_iota(jnp.int32, sums.shape, 0)
            tail = jnp.where(at == 1, sums[0:1] - top[0:1], top)
            return jnp.concatenate([part[:width], tail], axis=0).astype(bf16)
        return pack

    s6i_start, s6i_mid, s6i_fin = sum_mp(lambda q: r["g6i"].at[q], r["rc6i"], r["st6i"], r["rx6i"], img_sends, packer(IS))
    s6t_start, s6t_mid, s6t_fin = sum_mp(lambda q: r["g6t"].at[q], r["rc6t"], r["st6t"], r["rx6t"], txt_sends, packer(TS))
    spans = [slice(j * FC, (j + 1) * FC) for j in range(FI // FC)]
    whole_t = [slice(0, FT)]
    whole_j = [slice(0, TS)]
    def sb2(j, p):
        return r["w2"].at[pl.ds(pl.multiple_of(j * 8 * IO + p * 2 * IO, 2 * IO), 2 * IO), 0:FC]

    def sb1(j, p):
        return r["w1"].at[pl.ds(pl.multiple_of(p * 4 * IO, 4 * IO), 4 * IO), spans[j]]

    def sb1z(p):
        return r["w1"].at[pl.ds(pl.multiple_of(p * 2 * IO, 2 * IO), 2 * IO), spans[2]]

    w2_steps = scatter_dp(
        "z", IO, IP, spans, sb2, r["ra2"], r["sc2"], r["rc2"])
    w1_steps = scatter_dp(
        "y", IO, IP, spans[:2], sb1, r["ra1"], r["sc1"], r["rc1"])
    w1_steps += scatter_dp("z", IO, IP, [slice(0, FC)], lambda j, p: sb1z(p), r["ra1z"], r["sc1z"], r["rc1z"])
    t2_steps = scatter_dp("z", TO, TP, whole_t, lambda j, p: r["sbt2"].at[p], r["rat2"], r["sct2"], r["rct2"])
    t1_steps = scatter_dp("z", TO, TP, whole_t, lambda j, p: r["sbt1"].at[p], r["rat1"], r["sct1"], r["rct1"])
    pj_steps = scatter_dp("y", IO, IP, whole_j, lambda j, p: r["sbj"].at[p], r["raj"], r["scj"], r["rcj"])

    @pl.when(image)
    def _():
        load_xi.start()
        load_w1.start()
        load_w2.start()
        load_pj.start()

    @pl.when(text)
    def _():
        load_xt.start()
        load_t1.start()
        load_t2.start()

    barrier = pltpu.get_barrier_semaphore()
    partners = [sib, opp, diag, flip] + others_t + [(t, dd, m) for dd in others_d]
    for dev in partners:
        pl.semaphore_signal(barrier, inc=1, device_id=dev, device_id_type=MESH)
    pl.semaphore_wait(barrier, len(partners))

    @pl.when(image)
    def _():
        load_xi.wait()
        xi_start()
        r["labo"][...] = jnp.full((8, 128), label[0, 0].astype(f32))
        lab_up.start()
        load_pj.wait()
        pj_start()
        xi_mid()
        xi_fin()
        xt32 = r["xs"][...].astype(f32)
        inv = lax.rsqrt(jnp.sum(xt32 * xt32, axis=0, keepdims=True) / WI + epsilon)
        r["ivi"][...] = inv
        r["ns"][...] = (xt32 * inv).astype(bf16)
        nor_si()
        r["nf"][...] = r["ns"][...].T

    @pl.when(text)
    def _():
        load_xt.wait()
        xt_start()
        xt_mid()
        xt_fin()
        xt32 = r["xt"][...].astype(f32)
        inv = lax.rsqrt(jnp.sum(xt32 * xt32, axis=0, keepdims=True) / WT + epsilon)
        r["ivt"][...] = inv
        r["nt"][...] = (xt32 * inv).astype(bf16)
        nor_st()
        r["ntf"][...] = r["nt"][...].T

    @pl.when(image)
    def _():
        load_w1.wait()

        def front(j, carry):
            at = pl.ds(pl.multiple_of(j * 384, 384), 384)
            u = dot(r["nf"][...], r["w1"][:, at])
            val, slope = gelu_both(u)
            r["hi"][ti, :, at] = val.astype(bf16)
            r["gi"][:, at] = slope
            return carry

        lax.fori_loop(0, FI // 384, front, 0)

    @pl.when(text)
    def _():
        load_t1.wait()

        for at in (slice(0, 256), slice(256, 512), slice(512, 640)):
            val, slope = gelu_both(dot(r["ntf"][...], r["w1"][0:WT, at]))
            r["ht"][:, at] = val.astype(bf16)
            r["gt"][:, at] = slope

    @pl.when(image)
    def _():
        hid[0][0]()
        hid[1][0]()
        load_w2.wait()

        def back(j, carry):
            at = pl.ds(pl.multiple_of(j * 256, 256), 256)
            r["p2i"][:, at] = dot(r["hi"][ti], r["w2"][:, at])
            return carry

        lax.fori_loop(0, WI // 256, back, 0)

    @pl.when(text)
    def _():
        load_t2.wait()

        def back(j, carry):
            at = pl.ds(pl.multiple_of(j * 384, 384), 384)
            r["p2t"][:, at] = dot(r["ht"][...], r["w2"][0:FT, at])
            return carry

        lax.fori_loop(0, WT // 384, back, 0)
        for s in range(3):
            arrive(r["lab"].at[d, s], lab_b + s)
        for c in lab_out:
            c.start()

    @pl.when(image)
    def _():
        s2i_start()
        pj_mid()
        r["xf"][...] = r["xs"][...].T
        s2i_mid()
        part = s2i_fin()
        rows = pl.ds(pl.multiple_of(m * IQ, IQ), IQ)
        x = r["xf"][rows, :].astype(f32)
        blended = (x + (part + r["rx2i"][...].astype(f32))).astype(bf16)
        for k in range(NM):
            r["bl"][m, k] = blended[:, k * IS:(k + 1) * IS]
        pj_fin()
        projected = dot_t(blended, r["pj"][...])
        length = jnp.sqrt(jnp.sum(projected * projected, axis=1, keepdims=True))
        r["pr"][...] = projected
        r["ln"][...] = length
        r["ei"][m] = (projected / length).astype(bf16)
        star_img.start()
        ei_start()
        bl_start()

    @pl.when(text)
    def _():
        s2t_start()
        r["xtf"][...] = r["xt"][...].T
        s2t_mid()
        part = s2t_fin()
        rows = pl.ds(pl.multiple_of(m * TQ, TQ), TQ)
        x = r["xtf"][rows, :].astype(f32)
        blended = x + (part + r["rx2t"][...].astype(f32))
        length = jnp.sqrt(jnp.sum(blended * blended, axis=1, keepdims=True))
        r["tb"][...] = blended
        r["tl"][...] = length
        r["et"][m] = (blended / length).astype(bf16)
        for c in star_txt:
            c.start()
        et_start()

    for c in range(3):
        arrive(cols.at[d, pl.ds(IQ * c, IQ)], star + c)
        for copy in ring_out[c]:
            copy.start()

    @pl.when(image)
    def _():
        ei_mid()
        hid[2][0]()
        bl_mid()
        ei_fin()

    @pl.when(text)
    def _():
        et_mid()
        hid[0][1]()
        et_fin()
        for dd in others_d:
            arrive(r["lab"].at[dd], lab_d + dd)

    scale_v, bias_v, loss_v = scale[0, 0], bias[0, 0], loss[0, 0]

    def weight(scores, positive):
        logits = scale_v * scores + bias_v
        signed = jnp.where(positive, 1.0, -1.0).astype(f32)
        grad = -loss_v * signed * jax.nn.sigmoid(-signed * logits)
        return (scale_v * grad).astype(bf16)

    def block_ready(dd):
        for c in range(3):
            arrive(cols.at[dd, pl.ds(IQ * c, IQ)], ring + ND * c + dd)

    @pl.when(image)
    def _():
        emb = r["ei"][...].reshape(IR, WT)
        row = (t * ND + d) * IR + lax.broadcasted_iota(jnp.int32, (IR, TQ), 0) + label[0, 0]
        target = jnp.where(row >= BATCH, row - BATCH, row)
        lane = lax.broadcasted_iota(jnp.int32, (IR, TQ), 1)

        def block(dd):
            pw = weight(dot_t(emb, cols[dd]), target == lane + (dd * TR + m * TQ))
            return dot(pw, cols[dd])

        r["q4t"][0:IR] = block(d)

        def step(k, carry):
            dd = (d + k) % ND
            block_ready(dd)
            r["q4t"][0:IR] += block(dd)
            return carry

        lax.fori_loop(1, ND, step, 0)

    @pl.when(text)
    def _():
        emb = r["et"][...].reshape(TR, WT)
        row = d * TR + lax.broadcasted_iota(jnp.int32, (TR, TQ), 0)
        lane = lax.broadcasted_iota(jnp.int32, (1, TQ), 1)
        part = lane // IQ

        def block(dd):
            off = r["lab"][dd]
            off = jnp.where(part == 0, off[0, :1, :TQ], jnp.where(part == 1, off[1, :1, :TQ], off[2, :1, :TQ]))
            own = (part * ND + dd) * IR + m * IQ + lane % IQ
            target = own + off.astype(jnp.int32)
            target = jnp.where(target >= BATCH, target - BATCH, target)
            pw = weight(dot_t(emb, cols[dd]), row == target)
            return dot(pw, cols[dd])

        r["q4t"][...] = block(d)

        def step(k, carry):
            dd = (d + k) % ND
            block_ready(dd)
            r["q4t"][...] += block(dd)
            return carry

        lax.fori_loop(1, ND, step, 0)

    @pl.when(image)
    def _():
        s4i_start()
        s4i_mid()
        part = s4i_fin()
        grad = part + r["rx4t"][0:IQ].astype(f32)
        length = r["ln"][...]
        direction = r["pr"][...] / length
        pg = ((grad - direction * jnp.sum(direction * grad, axis=1, keepdims=True)) / length).astype(bf16)
        r["bfi"][m] = dot(pg, r["pj"][...]).astype(bf16)
        r["pgf"][...] = pg

    @pl.when(text)
    def _():
        s4t_start()
        s4t_mid()
        part = s4t_fin()
        grad = part + r["rx4t"][...].astype(f32)
        length = r["tl"][...]
        direction = r["tb"][...] / length
        blended_grad = (grad - direction * jnp.sum(direction * grad, axis=1, keepdims=True)) / length
        r["bft"][m] = blended_grad.astype(bf16)

    @pl.when(image)
    def _():
        bi_start()
        for k in range(NM):
            r["pgs"][k] = r["pgf"][:, k * TS:(k + 1) * TS]
        r["pgr"][m] = r["pgs"][m]
        for c in pg_out:
            c.start()
        bl_fin()
        blx_si()
        r["al"][ti] = r["bl"][:, ti]
        r["an"][ti] = r["ns"][pl.ds(pl.multiple_of(ti * IS, IS), IS), :]
        bi_mid()
        bi_fin()
        r["bsi"][...] = r["bfi"][...].reshape(IR, WI).T
        bg_si()
        r["ab"][ti] = r["bsi"][pl.ds(pl.multiple_of(ti * IS, IS), IS), :]

    @pl.when(text)
    def _():
        bt_start()
        r["ant"][...] = r["nt"][(NT - 1) * TS:]
        bt_mid()
        bt_fin()
        r["bst"][...] = r["bft"][...].reshape(TR, WT).T
        bg_st()
        r["abt"][...] = r["bst"][(NT - 1) * TS:]

    @pl.when(image)
    def _():
        for j in range(FI // FC):
            for lo, wide in ((0, 384), (384, 256)):
                at = slice(j * FC + lo, j * FC + lo + wide)
                hg = dot_t(r["bfi"][...].reshape(IR, WI), r["w2"][at, :])
                r["ki"][ti, :, at] = (hg * r["gi"][:, at]).astype(bf16)
            if j == 0:
                pre[0][0]()
        for dev in (opp, diag, sib):
            arrive(r["pgr"].at[dev[2]], pgb + dev[2])
        pgx_si()
        r["bj"][ti] = r["pgr"][...]

    @pl.when(text)
    def _():
        for at in (slice(0, 384), slice(384, 640)):
            hg = dot_t(r["bft"][...].reshape(TR, WT), r["w2"][at, 0:WT])
            r["kt"][:, at] = (hg * r["gt"][:, at]).astype(bf16)
        pre[0][1]()

    def by_z(g, own, dst, at):
        for p in range(4):
            pair = [g[(q * 4 + p) * own:(q * 4 + p + 1) * own] for q in range(2)]
            dst(p)[:, at] = jnp.concatenate(pair, axis=0).astype(bf16)

    def by_y(g, own, dst, at):
        for p in range(2):
            dst(p)[:, at] = g[p * 4 * own:(p + 1) * 4 * own].astype(bf16)

    def product(lhs, rhs, put, own, dst, begin, width):
        done = 0
        while done < width:
            wide = min(384, width - done)
            put(dot(lhs, rhs(slice(begin + done, begin + done + wide))), own, dst, slice(done, done + wide))
            done += wide

    def three(name):
        return jnp.concatenate([r[name][s] for s in range(3)], axis=1)

    bg_fin()
    for j in range(FI // FC):
        hid[j][2]()
        product(three("ab"), lambda at: r["hi"][:, :, at].reshape(3 * IR, at.stop - at.start),
                by_z, IO, lambda p, j=j: sb2(j, p), j * FC, FC)
        w2_steps[j][0]()
        if j == 1:
            @pl.when(image)
            def _():
                pre[1][0]()
    blx_fin()
    pgx_fin()
    by_y(dot_rows(r["al"][...].reshape(3 * IR, IS), r["bj"][...].reshape(3 * IR, TS)), IO,
         lambda p: r["sbj"].at[p], slice(0, TS))
    pj_steps[0][0]()
    product(r["abt"][...], lambda at: r["ht"][:, at], by_z, TO, lambda p: r["sbt2"].at[p], 0, FT)
    t2_steps[0][0]()

    @pl.when(image)
    def _():
        total = jnp.zeros((1, IR), f32)
        for k in range(NM):
            g = dot_t(r["w1"][k * IS:(k + 1) * IS, :], r["ki"][ti])
            total = total + jnp.sum(r["ns"][k * IS:(k + 1) * IS, :].astype(f32) * g, axis=0, keepdims=True)
            r["g6i"][k, 0:IS, :] = g
        tail = jnp.broadcast_to(total, (16, IR))
        for k in range(NM):
            r["g6i"][k, IS:IG, :] = tail
        s6i_start()
        pre[2][0]()

    @pl.when(text)
    def _():
        total = jnp.zeros((1, TR), f32)
        for k in range(NM):
            g = dot_t(r["w1"][k * TS:(k + 1) * TS, 0:FT], r["kt"][...])
            total = total + jnp.sum(r["nt"][k * TS:(k + 1) * TS, :].astype(f32) * g, axis=0, keepdims=True)
            r["g6t"][k, 0:TS, :] = g
        tail = jnp.broadcast_to(total, (16, TR))
        for k in range(NM):
            r["g6t"][k, TS:TG, :] = tail
        s6t_start()

    nor_fin()
    for j in range(FI // FC):
        pre[j][2]()
        product(three("an"), lambda at: r["ki"][:, :, at].reshape(3 * IR, at.stop - at.start),
                by_z if j == 2 else by_y, IO, (lambda p: sb1z(p)) if j == 2 else (lambda p, j=j: sb1(j, p)), j * FC, FC)
        w1_steps[j][0]()
        if j == 0:
            @pl.when(image)
            def _():
                s6i_mid()

            @pl.when(text)
            def _():
                s6t_mid()
            product(r["ant"][...], lambda at: r["kt"][:, at], by_z, TO, lambda p: r["sbt1"].at[p], 0, FT)
            t1_steps[0][0]()
        w2_steps[j][1]()
        if j == 1:
            t2_steps[0][1]()
            w1_steps[0][1]()
    w1_steps[1][1]()
    pj_steps[0][1]()

    @pl.when(image)
    def _():
        part = s6i_fin()
        other = r["rx6i"][...].astype(f32)
        average = (part[IS:IS + 1] + other[IS:IS + 1] + other[IS + 1:IS + 2]) / WI
        grad = part[:IS] + other[:IS]
        inv = r["ivi"][...]
        normed = r["xs"][mi, :].astype(f32) * inv
        o_img[0] = r["bsi"][mi, :].astype(f32) + (grad - normed * average) * inv
        o_txt[0] = jnp.zeros((TS, TR), f32)

    @pl.when(text)
    def _():
        part = s6t_fin()
        other = r["rx6t"][...].astype(f32)
        average = (part[TS:TS + 1] + other[TS:TS + 1] + other[TS + 1:TS + 2]) / WT
        grad = part[:TS] + other[:TS]
        inv = r["ivt"][...]
        normed = r["xt"][mt, :].astype(f32) * inv
        o_txt[0] = r["bst"][mt, :].astype(f32) + (grad - normed * average) * inv
        o_img[0] = jnp.zeros((IS, IR), f32)

    w1_steps[2][1]()
    t1_steps[0][1]()
    for j in range(FI // FC):
        w2_steps[j][2](o_w2)
    t2_steps[0][2](o_t2)
    pj_steps[0][2](o_pj)
    for j in range(FI // FC):
        w1_steps[j][2](o_w1, spans[j])
    t1_steps[0][2](o_t1)

    for c in all_sends:
        c.wait_send()

    @pl.when(image)
    def _():
        for c in img_sends:
            c.wait_send()

    @pl.when(text)
    def _():
        for c in txt_sends:
            c.wait_send()


def move(*refs):
    n = len(refs) // 2
    sem = refs[-1]
    copies = [pltpu.make_async_copy(refs[k], refs[n + k], sem.at[k]) for k in range(n)]
    for c in copies:
        c.start()
    for c in copies:
        c.wait()


def per_device(
    image_in, text_in, img_w1, img_w2, img_proj, txt_w1, txt_w2, label_offset,
    logit_scale, logit_bias, loss_scale,
):
    anywhere = pl.BlockSpec(memory_space=pl.ANY)
    scalar = pl.BlockSpec(memory_space=pltpu.SMEM)
    vmem = pl.BlockSpec(memory_space=pltpu.VMEM)
    one = lambda v: v.reshape(1, 1)
    outs = pl.pallas_call(
        step_kernel,
        out_shape=[
            jax.ShapeDtypeStruct((1, IS, IR), f32),
            jax.ShapeDtypeStruct((1, TS, TR), f32),
            jax.ShapeDtypeStruct((IO, FI), f32),
            jax.ShapeDtypeStruct((IO, FI), f32),
            jax.ShapeDtypeStruct((IO, TS), f32),
            jax.ShapeDtypeStruct((TO, FT), f32),
            jax.ShapeDtypeStruct((TO, FT), f32),
        ],
        in_specs=[anywhere] * 7 + [scalar] * 4,
        out_specs=[vmem] * 7,
        scratch_shapes=list(scratch_list().values()),
        compiler_params=pltpu.CompilerParams(
            collective_id=0, has_side_effects=True, vmem_limit_bytes=63 << 20
        ),
        name="step",
    )(
        image_in.swapaxes(1, 2), text_in.swapaxes(1, 2), img_w1, img_w2, img_proj.T, txt_w1, txt_w2, label_offset,
        one(logit_scale), one(logit_bias), one(loss_scale),
    )
    outs = pl.pallas_call(
        move,
        out_shape=[jax.ShapeDtypeStruct(o.shape, o.dtype) for o in outs],
        in_specs=[anywhere] * len(outs),
        out_specs=[vmem] * len(outs),
        scratch_shapes=[pltpu.SemaphoreType.DMA((len(outs),))],
        name="place",
    )(*outs)
    g_img, g_txt, g_w1, g_w2, g_pj, g_t1, g_t2 = outs
    return (g_img.swapaxes(1, 2), g_txt.swapaxes(1, 2), g_w1, g_w2.T, g_pj, g_t1, g_t2.T)


def solution(mesh):
    return jax.shard_map(
        per_device,
        mesh=mesh,
        in_specs=(
            P("tower", "dp", "mp"),
            P("tower", "dp", "mp"),
            P(None, "mp"),
            P("mp", None),
            P(None, "mp"),
            P(None, "mp"),
            P("mp", None),
            P("tower", "dp"),
            P(),
            P(),
            P(),
        ),
        out_specs=(
            P("tower", "dp", "mp"),
            P("tower", "dp", "mp"),
            P(("tower", "dp"), "mp"),
            P("mp", ("tower", "dp")),
            P(("tower", "dp"), "mp"),
            P(("tower", "dp"), "mp"),
            P("mp", ("tower", "dp")),
        ),
        check_vma=False,
    )
```
